512 devices in a mesh: enc: 16 (over z), seq: 8 (over x, core), tp: 4 (over y).
Axes of the slice: x: 4, y: 4, z: 16, core: 2. Of those that a mesh axis runs over, the one named last changes fastest.
Arguments:
- frames: bfloat16 [49152, 1280], P(('enc', 'seq'), 'tp'), may hold values from -6 to 6
- proj_weight: bfloat16 [1280, 8192], P('enc', 'tp'), may hold values from -0.15625 to 0.15625
- text_emb: bfloat16 [40960, 8192], P(('enc', 'seq'), 'tp')
- norm_gain: float32 [8192], P('tp'), may hold values from 0.1 to 1.9
- cotangent: bfloat16 [40960, 8192], P(('enc', 'seq'), 'tp'), may hold values from -6 to 6
- counts: int32 [128, 16], P(('enc', 'seq')), may hold values from 6 to 18, as said below
- offsets: int32 [128], P(('enc', 'seq')), may hold values from 0 to 32, as said below
Outputs:
- mixed: bfloat16 [40960, 8192], P(('enc', 'seq'), 'tp')
- grad_frames: bfloat16 [49152, 1280], P(('enc', 'seq'), 'tp')
The draws below stay inside these ranges and needn't reach their ends.
Inputs may be any that keep to these rules, and one draw needn't show every extreme that they name: Each row of counts sums to 192, so every pooled row is placed. In every draw some q has counts[r, q] = 18 for every r. offsets[b] plus the pooled rows that token block b receives never exceeds 320, and reaches it for some b.
All inputs are finite; a program needn't handle non-finite values.
Results may differ from the reference program's by a relative error of at most 0.0052.
Values may be sent and summed in bfloat16 or wider, within the bound.
A program may use at most 64 MiB of HBM per device.

```python
import math
import jax
import jax.numpy as jnp
from jax import lax

E = 1280
D = 8192
FR_DEV = 384
T_DEV = 320
FRAMES = 49152
TOKENS = 40960
N_ENC = 16
N_SEQ = 8


def shared_grid(key):
    block_rows = N_ENC * N_SEQ
    base = FR_DEV // 2 // N_ENC
    half = base // 2
    chosen = jax.random.randint(jax.random.fold_in(key, 12), (), 0, N_ENC).astype(jnp.int32)
    row_keys = jax.random.split(jax.random.fold_in(key, 11), block_rows)
    orders = jax.vmap(lambda one: jax.random.permutation(one, N_ENC))(row_keys).astype(jnp.int32)
    leading = orders[:, 0:1]
    orders = jnp.where(orders == chosen, leading, orders)
    orders = orders.at[:, 0].set(chosen).astype(jnp.int32)
    shifts = jax.random.randint(jax.random.fold_in(key, 13), (block_rows, N_ENC // 2), 0, half + 1).astype(jnp.int32)
    shifts = shifts.at[:, 0].set(half)
    paired = jnp.stack([shifts, -shifts], axis=2).reshape(block_rows, N_ENC)
    values = (base + paired).astype(jnp.int32)
    row_ids = jnp.arange(block_rows, dtype=jnp.int32)[:, None]
    grid = jnp.zeros((block_rows, N_ENC), jnp.int32).at[row_ids, orders].set(values)
    return (grid.reshape(N_ENC, N_SEQ, N_ENC).astype(jnp.int32), chosen)


def draw_counts(key, part):
    grid, chosen = shared_grid(key)
    return grid.reshape(N_ENC * N_SEQ, N_ENC).astype(jnp.int32)


def draw_offsets(key, part):
    grid, chosen = shared_grid(key)
    key = jax.random.fold_in(key, 5)
    arrived = jnp.sum(grid, axis=0).T.reshape(-1)
    top_offset = T_DEV - 3 * FR_DEV // 4
    room = jnp.minimum(T_DEV - arrived, top_offset).astype(jnp.int32)
    drawn = jax.random.randint(key, (N_ENC * N_SEQ,), 0, room + 1).astype(jnp.int32)
    block_index = jnp.arange(N_ENC * N_SEQ, dtype=jnp.int32)
    drawn = jnp.where(block_index == chosen * N_SEQ, top_offset, drawn)
    drawn = jnp.where(block_index == (chosen + 1) % N_ENC * N_SEQ, 0, drawn)
    return drawn.astype(jnp.int32)


def draw_text_emb(key, part):
    key = jax.random.fold_in(key, 7)
    first, second, third = jax.random.split(key, 3)
    rising = jnp.exp(math.log(3.0) * jnp.arange(D, dtype=jnp.float32) / D)
    column_scale = rising * jnp.exp(jax.random.uniform(second, (D,), jnp.float32, 0.0, math.log(4.0)))
    base = jax.random.normal(first, (TOKENS, D), jnp.float32)
    row_scale = jnp.exp(jax.random.uniform(third, (TOKENS, 1), jnp.float32, math.log(0.5), math.log(5.0)))
    return (base * column_scale * row_scale).astype(jnp.bfloat16)


def levels(own_key, shape, pieces, low, high):
    loudness, own = 1.0, jax.random.fold_in(own_key, 6)
    for dim, shards_of in pieces:
        draws = jnp.exp(jax.random.uniform(jax.random.fold_in(own, dim), (shards_of,), jnp.float32, low / len(pieces), high / len(pieces)))
        loudness = loudness * jnp.repeat(draws, shape[dim] // shards_of).reshape([-1 if axis == dim else 1 for axis in range(len(shape))])
    return loudness


def normal_values(key, shape, width, reach, cuts=(), held_as=jnp.bfloat16):
    gain = levels(key, shape, cuts, -0.22, 0.18) if cuts else 1.0
    values = jax.random.normal(key, shape, jnp.float32) * width * gain
    return jnp.minimum(jnp.maximum(values, -reach), reach).astype(held_as)


def setup_inputs(seed: int = 0) -> dict:
    key_list = jax.random.split(jax.random.key(seed), 8)
    frames = normal_values(key_list[0], (FRAMES, E), 1.0, 6.0, ((0, 128), (1, 4)))
    proj_weight = normal_values(key_list[1], (E, D), E ** -0.5, 0.15625, ((0, 16), (1, 4)))
    text_emb = draw_text_emb(jax.random.fold_in(key_list[7], 71), 0)
    norm_gain = jnp.clip(1.0 + 0.18 * jax.random.normal(key_list[3], (D,), jnp.float32), 0.1, 1.9)
    cotangent = normal_values(key_list[4], (TOKENS, D), 1.0, 6.0, ((0, 128), (1, 4)))
    counts = draw_counts(jax.random.fold_in(key_list[7], 71), 0)
    offsets = draw_offsets(jax.random.fold_in(key_list[7], 71), 0)
    return dict(frames=frames, proj_weight=proj_weight, text_emb=text_emb, norm_gain=norm_gain, cotangent=cotangent, counts=counts, offsets=offsets)


def reference(frames, proj_weight, text_emb, norm_gain, cotangent, counts, offsets):
    shard_count = N_ENC * N_SEQ
    pooled_rows = FR_DEV // 2
    framed = frames.reshape(shard_count * pooled_rows, 2, E).astype(jnp.float32)
    pooled = (lax.optimization_barrier(jnp.sum(framed, axis=1)) * 0.5).astype(jnp.bfloat16)
    projected = jnp.dot(pooled, proj_weight, preferred_element_type=jnp.float32).astype(jnp.bfloat16)
    row_start = (jnp.cumsum(counts, axis=1) - counts).astype(jnp.int32)
    row_end = (row_start + counts).astype(jnp.int32)
    frame_index = jnp.arange(pooled_rows, dtype=jnp.int32)
    target = lax.optimization_barrier(jnp.sum((row_end[:, None, :] <= frame_index[None, :, None]).astype(jnp.int32), axis=2)).astype(jnp.int32)
    usable = frame_index[None, :] < row_end[:, -1:]
    target = jnp.minimum(target, N_ENC - 1).astype(jnp.int32)
    within = frame_index[None, :] - jnp.take_along_axis(row_start, target, axis=1)
    grid = counts.reshape(N_ENC, N_SEQ, N_ENC)
    earlier = (jnp.cumsum(grid, axis=0) - grid).astype(jnp.int32).reshape(shard_count, N_ENC)
    column = (jnp.arange(shard_count, dtype=jnp.int32) % N_SEQ)[:, None]
    token_shard = (target * N_SEQ + column).astype(jnp.int32)
    position = token_shard * T_DEV + offsets[token_shard] + jnp.take_along_axis(earlier, target, axis=1) + within
    position = jnp.where(usable, position, TOKENS).astype(jnp.int32).reshape(-1)
    placed = jnp.zeros((TOKENS, D), jnp.bfloat16).at[position].set(projected, mode='drop')
    audio_mask = jnp.zeros((TOKENS, 1), jnp.float32).at[position].set(1.0, mode='drop')

    def normalize(block):
        text_rows, placed_rows, mask_rows, cot_rows = block
        hidden = jnp.where(mask_rows > 0.5, placed_rows.astype(jnp.float32), text_rows.astype(jnp.float32))
        inv_rms = lax.rsqrt(lax.optimization_barrier(jnp.sum(hidden * hidden, axis=1, keepdims=True)) / D + 1e-05)
        mixed = (hidden * inv_rms * norm_gain).astype(jnp.bfloat16)
        weighted = cot_rows.astype(jnp.float32) * norm_gain
        slope_term = lax.optimization_barrier(jnp.sum(weighted * hidden, axis=1, keepdims=True)) / D
        grad_hidden = (inv_rms * weighted - inv_rms ** 3 * hidden * slope_term).astype(jnp.bfloat16)
        return (mixed, grad_hidden)
    mixed, grad_hidden = lax.map(normalize, (text_emb.reshape(shard_count, T_DEV, D), placed.reshape(shard_count, T_DEV, D), audio_mask.reshape(shard_count, T_DEV, 1), cotangent.reshape(shard_count, T_DEV, D)))
    grad_rows = jnp.take(grad_hidden.reshape(TOKENS, D), position, axis=0, mode='fill', fill_value=0)
    grad_pooled = jnp.dot(grad_rows, proj_weight.T, preferred_element_type=jnp.float32).astype(jnp.bfloat16)
    halved = (grad_pooled.astype(jnp.float32) * 0.5)[:, None, :]
    grad_frames = jnp.broadcast_to(halved, (shard_count * pooled_rows, 2, E)).reshape(FRAMES, E).astype(jnp.bfloat16)
    return (mixed.reshape(TOKENS, D), grad_frames)
```

```python
import jax
import jax.numpy as jnp
from jax import lax
from jax.experimental import pallas as pl
from jax.experimental.pallas import tpu as pltpu
from jax.sharding import PartitionSpec as P

D = 8192
EPS = 1e-05
MESH = pl.DeviceIdType.MESH
F32 = jnp.float32
BF16 = jnp.bfloat16

N_ENC = 16
N_X = 4
N_TP = 4
CHUNK = 80
WIDE = 2048
PART = 320
SLAB = 512
HALF = 256
SLOT = 16
SLOTS = N_ENC * SLOT
LANES = 384
TOKENS = 320
HOPS = 8
STREAMS = ((0, 0), (1, 1), (0, 1), (1, 0))


def nt(a, b):
    return lax.dot_general(a, b, (((1,), (1,)), ((), ())), preferred_element_type=F32)


def nn(a, b):
    return jnp.dot(a, b, preferred_element_type=F32)


def identity(size):
    rows = lax.broadcasted_iota(jnp.int32, (size, size), 0)
    cols = lax.broadcasted_iota(jnp.int32, (size, size), 1)
    return (rows == cols).astype(F32).astype(BF16)


def slot_maps(start, count, target, value):
    place = jnp.bitwise_and(lax.broadcasted_iota(jnp.int32, target.shape, 0), SLOT - 1)
    placef = place.astype(F32)
    main = (start + placef == target) & (placef < count)
    extra = jnp.where(place >= 5, 17.0, 16.0)
    spare = (start + extra == target) & (extra < count) & (place < 10)
    zero = jnp.zeros_like(target)
    return jnp.where(main, value, zero).astype(BF16), jnp.where(spare, value, zero).astype(BF16)


def piece_mask(shape, axis, piece):
    place = jnp.bitwise_and(lax.broadcasted_iota(jnp.int32, shape, axis), SLOT - 1)
    return (place == piece) | (place == piece + 5)


def encode(main, spare, items):
    low = nt(main, items[0:256])
    none = jnp.zeros((64, items.shape[1]), BF16)
    high = nt(main, jnp.concatenate([items[256:320], none], axis=0))
    for piece in range(5):
        part = nt(spare, jnp.concatenate([none, items[64 * piece : 64 * piece + 64]], axis=0))
        high = high + jnp.where(piece_mask(part.shape, 0, piece), part, 0.0)
    return low, high


def decode(slots, main, spare, eye):
    turned = nt(eye, slots)
    rest = turned[320:384]
    pieces = [jnp.where(piece_mask(rest.shape, 1, piece), rest, 0.0) for piece in range(5)]
    stacked = jnp.concatenate(pieces, axis=0).astype(BF16)
    return nn(turned[0:320].astype(BF16), main) + nn(stacked, spare)


def column(row, size):
    return jnp.transpose(jnp.broadcast_to(row, (128, size)))


def kernel(
    frames, weight, text, gain, cot, counts, offset, mixed, grads,
    wfull, textv, cotv, hid, gh, mixv, turned, pooled, slots, ygat, ysend, yrecv, stats, sums, bsend, bret, fmap, tmap,
    zs, zr, xs, xr, as_, ar, bs, br, fs, fr, ys, yr, ss, sr, rs, rr, gs, gr, ls,
):
    e, s, t = lax.axis_index("enc"), lax.axis_index("seq"), lax.axis_index("tp")
    core = lax.rem(s, 2)
    chip = lax.div(s, 2)
    other = s + 1 - 2 * core
    x_next = lax.rem(chip + 1, N_X) * 2 + core
    x_prev = lax.rem(chip + N_X - 1, N_X) * 2 + core
    side = lax.rem(chip, 2)
    my_col = pl.multiple_of((side * 2 + core) * SLAB, SLAB)
    x_col = pl.multiple_of(((1 - side) * 2 + core) * SLAB, SLAB)

    def enc_at(step):
        return lax.rem(e + step + 2 * N_ENC, N_ENC)

    def tp_at(step):
        return lax.rem(t + step, N_TP)

    barrier = pltpu.get_barrier_semaphore()

    def greet(step, carry):
        pl.semaphore_signal(barrier, inc=1, device_id={"enc": enc_at(step)}, device_id_type=MESH)
        return carry

    lax.fori_loop(1, N_ENC, greet, 0)
    for step in range(1, N_TP):
        pl.semaphore_signal(barrier, inc=1, device_id={"tp": tp_at(step)}, device_id_type=MESH)
    for peer in (other, x_next, x_prev):
        pl.semaphore_signal(barrier, inc=1, device_id={"seq": peer}, device_id_type=MESH)

    own_rows = pl.ds(pl.multiple_of(e * CHUNK, CHUNK), CHUNK)
    locals_in = [
        pltpu.make_async_copy(weight, wfull.at[own_rows, :], ls.at[0]),
        pltpu.make_async_copy(text, textv, ls.at[1]),
        pltpu.make_async_copy(cot, cotv, ls.at[2]),
    ]
    for copy in locals_in:
        copy.start()

    row = lax.broadcasted_iota(jnp.int32, (SLOTS, N_ENC), 0)
    lane = lax.broadcasted_iota(jnp.int32, (SLOTS, N_ENC), 1)
    dealt = jnp.broadcast_to(counts[...].astype(F32), (SLOTS, N_ENC))
    block = jnp.right_shift(row, 4)
    count = jnp.sum(jnp.where(lane == block, dealt, 0.0), axis=1, keepdims=True)
    start = jnp.sum(jnp.where(lane < block, dealt, 0.0), axis=1, keepdims=True)
    target = jnp.right_shift(lax.broadcasted_iota(jnp.int32, (SLOTS, LANES), 1), 1).astype(F32)
    main, spare = slot_maps(start, count, target, 0.5)
    fmap[0] = main
    fmap[1] = spare
    low, high = encode(main, spare, frames[...])
    place = jnp.bitwise_and(lax.broadcasted_iota(jnp.int32, high.shape, 0), SLOT - 1)
    in_spare = lax.broadcasted_iota(jnp.int32, high.shape, 1) >= 64
    high = jnp.where((place >= 10) & in_spare, count, high)
    slots[:, 0:256] = low.astype(BF16)
    slots[:, 256:384] = high.astype(BF16)

    pl.semaphore_wait(barrier, N_ENC - 1 + N_TP - 1 + 3)

    def chunk_at(direction, hop):
        step = -(hop + 1) if direction == 0 else hop + 1
        return pl.ds(pl.multiple_of(enc_at(step) * CHUNK, CHUNK), CHUNK)

    def sem_at(direction, half, hop):
        return (direction * 2 + half) * HOPS + hop

    def z_copy(direction, half, hop, src, dst):
        index = sem_at(direction, half, hop)
        to = enc_at(1) if direction == 0 else enc_at(-1)
        return pltpu.make_async_remote_copy(
            src_ref=src, dst_ref=dst, send_sem=zs.at[index], recv_sem=zr.at[index],
            device_id={"enc": to}, device_id_type=MESH,
        )

    def seq_copy(ref, send, recv, index, to):
        return pltpu.make_async_remote_copy(
            src_ref=ref, dst_ref=ref, send_sem=send.at[index], recv_sem=recv.at[index],
            device_id={"seq": to}, device_id_type=MESH,
        )

    def own_slab(half):
        return pl.ds(pl.multiple_of(my_col + half * HALF, HALF), HALF)

    def x_slab(half):
        return pl.ds(pl.multiple_of(x_col + half * HALF, HALF), HALF)

    def first_hop(direction, half):
        return z_copy(direction, half, 0, weight.at[:, own_slab(half)], wfull.at[own_rows, own_slab(half)])

    def next_hop(direction, half, hop):
        ref = wfull.at[chunk_at(direction, hop - 1), own_slab(half)]
        return z_copy(direction, half, hop, ref, ref)

    def landed(direction, half, hop):
        ref = wfull.at[chunk_at(direction, hop), own_slab(half)]
        return z_copy(direction, half, hop, ref, ref)

    def x_copy(direction, half, hop):
        ref = wfull.at[chunk_at(direction, hop), own_slab(half)]
        return seq_copy(ref, xs, xr, sem_at(direction, half, hop), x_next if half == 0 else x_prev)

    def x_landed(direction, half, hop):
        ref = wfull.at[chunk_at(direction, hop), x_slab(half)]
        return seq_copy(ref, xs, xr, sem_at(direction, half, hop), x_next if half == 0 else x_prev)

    def core_copy(direction, half, hop):
        ref = wfull.at[chunk_at(direction, hop), own_slab(half)]
        return seq_copy(ref, as_, ar, sem_at(direction, half, hop), other)

    def core_relay(direction, half, hop):
        ref = wfull.at[chunk_at(direction, hop), x_slab(half)]
        return seq_copy(ref, bs, br, sem_at(direction, half, hop), other)

    def slot_rows(index):
        return pl.ds(pl.multiple_of(index * SLOT, SLOT), SLOT)

    def pooled_copy(step):
        return pltpu.make_async_remote_copy(
            src_ref=slots.at[slot_rows(enc_at(step)), :], dst_ref=ygat.at[t, slot_rows(e), :],
            send_sem=fs.at[step], recv_sem=fr.at[step], device_id={"enc": enc_at(step)}, device_id_type=MESH,
        )

    def pooled_landed(step):
        ref = ygat.at[t, slot_rows(enc_at(-step)), :]
        return pltpu.make_async_remote_copy(
            src_ref=ref, dst_ref=ref, send_sem=fs.at[step], recv_sem=fr.at[step],
            device_id={"enc": enc_at(step)}, device_id_type=MESH,
        )

    def each(low_step, high_step, do):
        def body(step, carry):
            do(step)
            return carry

        lax.fori_loop(low_step, high_step, body, 0)

    for direction, half in STREAMS:
        first_hop(direction, half).start()
    each(1, N_ENC, lambda step: pooled_copy(step).start())
    ygat[t, slot_rows(e), :] = slots[slot_rows(e), :]

    def arrive(hop, streams, onward):
        for direction, half in streams:
            landed(direction, half, hop).wait_recv()
            if (direction, half) in onward:
                next_hop(direction, half, hop + 1).start()
            x_copy(direction, half, hop).start()
            core_copy(direction, half, hop).start()

    def relay(hop, streams):
        for direction, half in streams:
            x_landed(direction, half, hop).wait_recv()
            core_relay(direction, half, hop).start()

    arrive(0, STREAMS, STREAMS)

    def ring(hop):
        arrive(hop, STREAMS, STREAMS)
        relay(hop - 1, STREAMS)

    each(1, 3, ring)

    each(1, N_ENC, lambda step: pooled_landed(step).wait_recv())

    def part_copy(step):
        return pltpu.make_async_remote_copy(
            src_ref=ygat.at[t], dst_ref=ygat.at[t], send_sem=ys.at[step], recv_sem=yr.at[step],
            device_id={"tp": tp_at(step)}, device_id_type=MESH,
        )

    def part_landed(step):
        ref = ygat.at[tp_at(N_TP - step)]
        return pltpu.make_async_remote_copy(
            src_ref=ref, dst_ref=ref, send_sem=ys.at[step], recv_sem=yr.at[step],
            device_id={"tp": tp_at(step)}, device_id_type=MESH,
        )

    for step in (2, 1, 3):
        part_copy(step).start()
    each(3, HOPS - 2, ring)
    arrive(HOPS - 2, STREAMS, STREAMS[:2])
    relay(HOPS - 3, STREAMS)

    slot = lax.broadcasted_iota(jnp.int32, (SLOTS, SLOTS), 0)
    source = lax.broadcasted_iota(jnp.int32, (SLOTS, SLOTS), 1)
    last = jnp.bitwise_and(source, SLOT - 1) == SLOT - 1
    slot_of, source_of = jnp.right_shift(slot, 4), jnp.right_shift(source, 4)
    same = jnp.where((slot_of == source_of) & last, 1.0, 0.0).astype(BF16)
    before = jnp.where((source_of < slot_of) & last, 1.0, 0.0).astype(BF16)
    marks = ygat[t, :, 256:384]
    end_lane = lax.broadcasted_iota(jnp.int32, (SLOTS, 128), 1) == 127
    count = jnp.sum(jnp.where(end_lane, nn(same, marks), 0.0), axis=1, keepdims=True)
    start = jnp.sum(jnp.where(end_lane, nn(before, marks), 0.0), axis=1, keepdims=True)
    first = offset[0].astype(F32)
    end = jnp.max(start + count, axis=0, keepdims=True) + first
    target = lax.broadcasted_iota(jnp.int32, (SLOTS, LANES), 1).astype(F32) - first
    main, spare = slot_maps(start, count, target, 1.0)
    tmap[0] = main
    tmap[1] = spare

    for step in range(1, N_TP):
        part_landed(step).wait_recv()
    eye = identity(LANES)
    for part in range(N_TP):
        turned[PART * part : PART * part + PART, :] = decode(ygat[part], main, spare, eye).astype(BF16)
    pooled[...] = nt(eye, turned[...]).astype(BF16)

    arrive(HOPS - 1, STREAMS[:2], ())
    relay(HOPS - 2, STREAMS)
    relay(HOPS - 1, STREAMS[:2])

    def seq_waits(hop, streams):
        for direction, half in streams:
            core_copy_in = wfull.at[chunk_at(direction, hop), own_slab(half)]
            seq_copy(core_copy_in, as_, ar, sem_at(direction, half, hop), other).wait_recv()
            seq_copy(core_copy_in, bs, br, sem_at(direction, half, hop), other).wait_recv()

    each(0, HOPS - 1, lambda hop: seq_waits(hop, STREAMS))
    seq_waits(HOPS - 1, STREAMS[:2])
    for copy in locals_in:
        copy.wait()

    sums[...] = jnp.zeros_like(sums)

    def forward(index):
        cols = pl.ds(pl.multiple_of(index * HALF, HALF), HALF)
        projected = nn(pooled[0:TOKENS, :], wfull[:, cols]).astype(BF16).astype(F32)
        token = lax.broadcasted_iota(jnp.int32, projected.shape, 0).astype(F32)
        hidden = jnp.where((token >= first) & (token < end), projected, textv[:, cols].astype(F32))
        hid[:, cols] = hidden.astype(BF16)
        squares = hidden * hidden
        slopes = cotv[:, cols].astype(F32) * gain[:, cols] * hidden
        sums[0, 0:TOKENS, :] += squares[:, 0:128] + squares[:, 128:256]
        sums[1, 0:TOKENS, :] += slopes[:, 0:128] + slopes[:, 128:256]

    each(0, WIDE // HALF, forward)

    stats[0] = jnp.zeros((8, LANES), F32)
    stats[0, 0:1, :] = jnp.sum(jnp.transpose(sums[0]), axis=0, keepdims=True)
    stats[0, 1:2, :] = jnp.sum(jnp.transpose(sums[1]), axis=0, keepdims=True)

    def stat_copy(step):
        return pltpu.make_async_remote_copy(
            src_ref=stats.at[0], dst_ref=stats.at[step], send_sem=ss.at[step], recv_sem=sr.at[step],
            device_id={"tp": tp_at(step)}, device_id_type=MESH,
        )

    for step in (2, 1, 3):
        stat_copy(step).start()
    gh[TOKENS:LANES, :] = jnp.zeros((LANES - TOKENS, WIDE), BF16)
    for step in (2, 1, 3):
        stat_copy(step).wait_recv()
    total = (stats[0] + stats[1]) + (stats[2] + stats[3])
    inv_row = lax.rsqrt(total[0:1] / D + EPS)
    slope_row = total[1:2] / D
    inv = column(inv_row, LANES)[0:TOKENS, 0:1]
    back = column(inv_row * inv_row * inv_row * slope_row, LANES)[0:TOKENS, 0:1]

    def backward(index):
        cols = pl.ds(pl.multiple_of(index * HALF, HALF), HALF)
        hidden = hid[:, cols].astype(F32)
        gains = gain[:, cols]
        weighted = cotv[:, cols].astype(F32) * gains
        gh[0:TOKENS, cols] = (inv * weighted - back * hidden).astype(BF16)
        mixv[:, cols] = (hidden * inv * gains).astype(BF16)

    each(0, WIDE // HALF, backward)
    mixed_out = pltpu.make_async_copy(mixv, mixed, ls.at[3])
    mixed_out.start()

    def sum_copy(step):
        return pltpu.make_async_remote_copy(
            src_ref=ysend.at[step], dst_ref=yrecv.at[step], send_sem=rs.at[step], recv_sem=rr.at[step],
            device_id={"tp": tp_at(step)}, device_id_type=MESH,
        )

    main, spare = tmap[0], tmap[1]
    for step in (2, 1, 3, 0):
        rows = pl.ds(pl.multiple_of(tp_at(step) * PART, PART), PART)
        partial = nt(wfull[rows, :], gh[...]).astype(BF16)
        low, high = encode(main, spare, partial)
        ysend[step, :, 0:256] = low.astype(BF16)
        ysend[step, :, 256:384] = high.astype(BF16)
        if step:
            sum_copy(step).start()
    for step in (2, 1, 3):
        sum_copy(step).wait_recv()
    bsend[...] = (
        (ysend[0].astype(F32) + yrecv[1].astype(F32)) + (yrecv[2].astype(F32) + yrecv[3].astype(F32))
    ).astype(BF16)

    def back_copy(step):
        return pltpu.make_async_remote_copy(
            src_ref=bsend.at[slot_rows(enc_at(step)), :], dst_ref=bret.at[slot_rows(e), :],
            send_sem=gs.at[step], recv_sem=gr.at[step], device_id={"enc": enc_at(step)}, device_id_type=MESH,
        )

    def back_landed(step):
        ref = bret.at[slot_rows(enc_at(-step)), :]
        return pltpu.make_async_remote_copy(
            src_ref=ref, dst_ref=ref, send_sem=gs.at[step], recv_sem=gr.at[step],
            device_id={"enc": enc_at(step)}, device_id_type=MESH,
        )

    each(1, N_ENC, lambda step: back_copy(step).start())
    bret[slot_rows(e), :] = bsend[slot_rows(e), :]

    def sent(hop, streams):
        for direction, half in streams:
            landed(direction, half, hop).wait_send()
            x_copy(direction, half, hop).wait_send()
            core_copy(direction, half, hop).wait_send()
            core_relay(direction, half, hop).wait_send()

    each(0, HOPS - 1, lambda hop: sent(hop, STREAMS))
    sent(HOPS - 1, STREAMS[:2])
    each(1, N_ENC, lambda step: pooled_copy(step).wait_send())
    for step in range(1, N_TP):
        part_copy(step).wait_send()
        stat_copy(step).wait_send()
        sum_copy(step).wait_send()

    each(1, N_ENC, lambda step: back_landed(step).wait_recv())
    grads[...] = decode(bret[...], fmap[0], fmap[1], identity(LANES)).astype(BF16)
    each(1, N_ENC, lambda step: back_copy(step).wait_send())
    mixed_out.wait()


def body(frames, proj_weight, text_emb, norm_gain, cotangent, counts, offsets):
    any_space = pl.BlockSpec(memory_space=pl.ANY)
    vmem = pl.BlockSpec(memory_space=pltpu.VMEM)
    smem = pl.BlockSpec(memory_space=pltpu.SMEM)
    dma = pltpu.SemaphoreType.DMA
    mixed, grads = pl.pallas_call(
        kernel,
        out_shape=(
            jax.ShapeDtypeStruct((TOKENS, WIDE), BF16),
            jax.ShapeDtypeStruct((PART, LANES), BF16),
        ),
        in_specs=[vmem, any_space, any_space, vmem, any_space, vmem, smem],
        out_specs=(any_space, vmem),
        scratch_shapes=[
            pltpu.VMEM((N_ENC * CHUNK, WIDE), BF16),
            pltpu.VMEM((TOKENS, WIDE), BF16),
            pltpu.VMEM((TOKENS, WIDE), BF16),
            pltpu.VMEM((TOKENS, WIDE), BF16),
            pltpu.VMEM((LANES, WIDE), BF16),
            pltpu.VMEM((TOKENS, WIDE), BF16),
            pltpu.VMEM((N_ENC * CHUNK, LANES), BF16),
            pltpu.VMEM((LANES, N_ENC * CHUNK), BF16),
            pltpu.VMEM((SLOTS, LANES), BF16),
            pltpu.VMEM((N_TP, SLOTS, LANES), BF16),
            pltpu.VMEM((N_TP, SLOTS, LANES), BF16),
            pltpu.VMEM((N_TP, SLOTS, LANES), BF16),
            pltpu.VMEM((N_TP, 8, LANES), F32),
            pltpu.VMEM((2, LANES, 128), F32),
            pltpu.VMEM((SLOTS, LANES), BF16),
            pltpu.VMEM((SLOTS, LANES), BF16),
            pltpu.VMEM((2, SLOTS, LANES), BF16),
            pltpu.VMEM((2, SLOTS, LANES), BF16),
            *[dma((4 * HOPS,)) for _ in range(8)],
            *[dma((N_ENC,)) for _ in range(2)],
            *[dma((N_TP,)) for _ in range(6)],
            *[dma((N_ENC,)) for _ in range(2)],
            dma((4,)),
        ],
        compiler_params=pltpu.CompilerParams(
            collective_id=0, has_side_effects=True, vmem_limit_bytes=56 * 1024 * 1024
        ),
    )(frames.T, proj_weight, text_emb, norm_gain.reshape(1, WIDE), cotangent, counts, offsets)
    return mixed, grads.T


def solution(mesh):
    in_specs = (
        P(("enc", "seq"), "tp"),
        P("enc", "tp"),
        P(("enc", "seq"), "tp"),
        P("tp"),
        P(("enc", "seq"), "tp"),
        P(("enc", "seq"), None),
        P(("enc", "seq")),
    )
    out_specs = (P(("enc", "seq"), "tp"), P(("enc", "seq"), "tp"))
    return jax.shard_map(body, mesh=mesh, in_specs=in_specs, out_specs=out_specs, check_vma=False)
```

```python
import jax
import jax.numpy as jnp
from jax import lax
from jax.experimental import pallas as pl
from jax.experimental.pallas import tpu as pltpu
from jax.sharding import PartitionSpec as P

D = 8192
EPS = 1e-05
MESH = pl.DeviceIdType.MESH
F32 = jnp.float32
BF16 = jnp.bfloat16

N_ENC = 16
N_X = 4
N_TP = 4
CHUNK = 80
WIDE = 2048
PART = 320
SLAB = 256
HALF = 128
SLOT = 16
SLOTS = N_ENC * SLOT
LANES = 384
TOKENS = 320
STAGES = 4
CLASSES = 4
GROUP = SLOTS // CLASSES


def nt(a, b):
    return lax.dot_general(a, b, (((1,), (1,)), ((), ())), preferred_element_type=F32)


def nn(a, b):
    return jnp.dot(a, b, preferred_element_type=F32)


def identity(size):
    rows = lax.broadcasted_iota(jnp.int32, (size, size), 0)
    cols = lax.broadcasted_iota(jnp.int32, (size, size), 1)
    return (rows == cols).astype(F32).astype(BF16)


def slot_maps(start, count, target, value):
    place = jnp.bitwise_and(lax.broadcasted_iota(jnp.int32, target.shape, 0), SLOT - 1)
    placef = place.astype(F32)
    main = (start + placef == target) & (placef < count)
    extra = jnp.where(place >= 5, 17.0, 16.0)
    spare = (start + extra == target) & (extra < count) & (place < 10)
    zero = jnp.zeros_like(target)
    return jnp.where(main, value, zero).astype(BF16), jnp.where(spare, value, zero).astype(BF16)


def piece_mask(shape, axis, piece):
    place = jnp.bitwise_and(lax.broadcasted_iota(jnp.int32, shape, axis), SLOT - 1)
    return (place == piece) | (place == piece + 5)


def distance(place):
    return jnp.bitwise_and(place, 3) * 4 + jnp.right_shift(place, 2)


def encode(main, spare, items):
    low = nt(main, items[0:256])
    none = jnp.zeros((64, items.shape[1]), BF16)
    high = nt(main, jnp.concatenate([items[256:320], none], axis=0))
    for piece in range(5):
        part = nt(spare, jnp.concatenate([none, items[64 * piece : 64 * piece + 64]], axis=0))
        high = high + jnp.where(piece_mask(part.shape, 0, piece), part, 0.0)
    return low, high


def decode(slots, main, spare, eye):
    turned = nt(eye, slots)
    rest = turned[320:384]
    pieces = [jnp.where(piece_mask(rest.shape, 1, piece), rest, 0.0) for piece in range(5)]
    stacked = jnp.concatenate(pieces, axis=0).astype(BF16)
    return nn(turned[0:320].astype(BF16), main) + nn(stacked, spare)


def column(row, size):
    return jnp.transpose(jnp.broadcast_to(row, (128, size)))


def kernel(
    frames_in, weight, text, gain_in, cot, counts_in, offset, mixed, grads,
    frames, gain, counts, wfull, textv, cotv, hid, gh, mixv, turned, pooled, slots, ygat, ysend, yrecv, stats, sums, bsend, bret, fmap, tmap,
    zs, zr, xs, xr, us, ur, cs, cr, fs, fr, ys, yr, ss, sr, rs, rr, gs, gr, ls,
):
    e, s, t = lax.axis_index("enc"), lax.axis_index("seq"), lax.axis_index("tp")
    core = lax.rem(s, 2)
    chip = lax.div(s, 2)
    other = s + 1 - 2 * core
    x_next = lax.rem(chip + 1, N_X) * 2 + core
    x_prev = lax.rem(chip + N_X - 1, N_X) * 2 + core

    def slab_at(step, which):
        return pl.multiple_of((lax.rem(chip + step, N_X) * 2 + which) * SLAB, SLAB)

    def enc_at(step):
        return lax.rem(e + step + 2 * N_ENC, N_ENC)

    def tp_at(step):
        return lax.rem(t + step, N_TP)

    barrier = pltpu.get_barrier_semaphore()

    def greet(step, carry):
        pl.semaphore_signal(barrier, inc=1, device_id={"enc": enc_at(step)}, device_id_type=MESH)
        return carry

    lax.fori_loop(1, N_ENC, greet, 0)
    for step in range(1, N_TP):
        pl.semaphore_signal(barrier, inc=1, device_id={"tp": tp_at(step)}, device_id_type=MESH)
    for peer in (other, x_next, x_prev):
        pl.semaphore_signal(barrier, inc=1, device_id={"seq": peer}, device_id_type=MESH)

    locals_in = [
        pltpu.make_async_copy(weight, wfull.at[0:CHUNK, :], ls.at[0]),
        pltpu.make_async_copy(text, textv, ls.at[1]),
        pltpu.make_async_copy(cot, cotv, ls.at[2]),
        pltpu.make_async_copy(gain_in, gain, ls.at[6]),
    ]
    first_in = [
        pltpu.make_async_copy(counts_in, counts, ls.at[4]),
        pltpu.make_async_copy(frames_in, frames, ls.at[5]),
    ]
    for copy in first_in:
        copy.start()

    pl.semaphore_wait(barrier, N_ENC - 1 + N_TP - 1 + 3)

    def chunk_rows(direction, far):
        return pl.ds(((N_ENC - far) if direction == 0 else far) * CHUNK, CHUNK)

    my_cols = pl.ds(slab_at(0, core), SLAB)

    def z_copy(direction, base, step):
        src = wfull.at[chunk_rows(direction, base), my_cols] if base else weight.at[:, my_cols]
        index = direction * 8 + base + step - 1
        return pltpu.make_async_remote_copy(
            src_ref=src, dst_ref=wfull.at[chunk_rows(direction, base + step), my_cols],
            send_sem=zs.at[index], recv_sem=zr.at[index],
            device_id={"enc": enc_at(step if direction == 0 else -step)}, device_id_type=MESH,
        )

    def reaches(direction, far):
        return far <= (8 if direction == 0 else 7)

    def z_sends(direction, base):
        for step in (2, 1):
            if reaches(direction, base + step):
                z_copy(direction, base, step).start()

    def z_landed(direction, far):
        step = 2 if far % 2 == 0 else 1
        z_copy(direction, far - step, step).wait_recv()

    def group_rows(direction, stage):
        if direction == 0:
            return pl.ds((N_ENC - 2 - 2 * stage) * CHUNK, 2 * CHUNK)
        return pl.ds((2 * stage + 1) * CHUNK, (2 if stage < STAGES - 1 else 1) * CHUNK)

    def seq_copy(ref, send, recv, index, to):
        return pltpu.make_async_remote_copy(
            src_ref=ref, dst_ref=ref, send_sem=send.at[index], recv_sem=recv.at[index],
            device_id={"seq": to}, device_id_type=MESH,
        )

    def x_copy(way, direction, stage):
        index = (way * 2 + direction) * STAGES + stage
        ref = wfull.at[group_rows(direction, stage), my_cols]
        return seq_copy(ref, xs, xr, index, x_next if way == 0 else x_prev)

    def x_landed(way, direction, stage):
        index = (way * 2 + direction) * STAGES + stage
        ref = wfull.at[group_rows(direction, stage), pl.ds(slab_at(3 if way == 0 else 1, core), SLAB)]
        seq_copy(ref, xs, xr, index, x_next if way == 0 else x_prev).wait_recv()

    def x_onward(way, direction, stage):
        index = (way * 2 + direction) * STAGES + stage
        cols = pl.ds(pl.multiple_of(slab_at(3 if way == 0 else 1, core) + way * HALF, HALF), HALF)
        return seq_copy(wfull.at[group_rows(direction, stage), cols], us, ur, index, x_next if way == 0 else x_prev)

    def far_landed(way, direction, stage):
        index = (way * 2 + direction) * STAGES + stage
        cols = pl.ds(pl.multiple_of(slab_at(2, core) + way * HALF, HALF), HALF)
        ref = wfull.at[group_rows(direction, stage), cols]
        seq_copy(ref, us, ur, index, x_next if way == 0 else x_prev).wait_recv()

    def core_copy(step, direction, stage, which):
        index = (step * 2 + direction) * STAGES + stage
        ref = wfull.at[group_rows(direction, stage), pl.ds(slab_at(step, which), SLAB)]
        return seq_copy(ref, cs, cr, index, other)

    def slot_rows(place):
        return pl.ds(pl.multiple_of(place * SLOT, SLOT), SLOT)

    def place_of(step):
        return lax.rem(step, 4) * 4 + lax.div(step, 4)

    def class_steps(kind):
        return (1 if kind == 0 else 0, 4), lambda index: 4 * index + kind

    def pooled_copy(step):
        return pltpu.make_async_remote_copy(
            src_ref=slots.at[slot_rows(place_of(step)), :],
            dst_ref=ygat.at[t, slot_rows(place_of(N_ENC - step)), :],
            send_sem=fs.at[step], recv_sem=fr.at[step], device_id={"enc": enc_at(step)}, device_id_type=MESH,
        )

    def pooled_landed(step):
        ref = ygat.at[t, slot_rows(place_of(N_ENC - step)), :]
        return pltpu.make_async_remote_copy(
            src_ref=ref, dst_ref=ref, send_sem=fs.at[step], recv_sem=fr.at[step],
            device_id={"enc": enc_at(step)}, device_id_type=MESH,
        )

    def each(low_step, high_step, do):
        def body(step, carry):
            do(step)
            return carry

        lax.fori_loop(low_step, high_step, body, 0)

    def each_of(kind, do):
        (low_index, high_index), step_of = class_steps(kind)
        each(low_index, high_index, lambda index: do(step_of(index)))

    for direction in (0, 1):
        z_sends(direction, 0)

    for copy in first_in:
        copy.wait()
    row = lax.broadcasted_iota(jnp.int32, (SLOTS, N_ENC), 0)
    lane = lax.broadcasted_iota(jnp.int32, (SLOTS, N_ENC), 1)
    dealt = jnp.broadcast_to(counts[...].astype(F32), (SLOTS, N_ENC))
    block = jnp.bitwise_and(distance(jnp.right_shift(row, 4)) + e, N_ENC - 1)
    count = jnp.sum(jnp.where(lane == block, dealt, 0.0), axis=1, keepdims=True)
    start = jnp.sum(jnp.where(lane < block, dealt, 0.0), axis=1, keepdims=True)
    target = jnp.right_shift(lax.broadcasted_iota(jnp.int32, (SLOTS, LANES), 1), 1).astype(F32)
    main, spare = slot_maps(start, count, target, 0.5)
    fmap[0] = main
    fmap[1] = spare
    low, high = encode(main, spare, frames[...])
    place = jnp.bitwise_and(lax.broadcasted_iota(jnp.int32, high.shape, 0), SLOT - 1)
    in_spare = lax.broadcasted_iota(jnp.int32, high.shape, 1) >= 64
    high = jnp.where((place >= 10) & in_spare, count, high)
    slots[:, 0:256] = low.astype(BF16)
    slots[:, 256:384] = high.astype(BF16)
    ygat[t, 0:SLOT, :] = slots[0:SLOT, :]

    def z_relay(stage):
        for direction in (0, 1):
            if reaches(direction, 2 * stage + 2):
                z_landed(direction, 2 * stage + 2)
                z_sends(direction, 2 * stage + 2)

    def seq_sends(stage):
        for direction in (0, 1):
            z_landed(direction, 2 * stage + 1)
            for way in (0, 1):
                x_copy(way, direction, stage).start()
            core_copy(0, direction, stage, core).start()

    def pooled_sends(kind):
        each_of(kind, lambda step: pooled_copy(step).start())

    def x_relay(stage):
        for direction in (0, 1):
            for way in (0, 1):
                x_landed(way, direction, stage)
                x_onward(way, direction, stage).start()
                core_copy(3 if way == 0 else 1, direction, stage, core).start()

    def far_relay(stage):
        for direction in (0, 1):
            for way in (0, 1):
                far_landed(way, direction, stage)
            core_copy(2, direction, stage, core).start()

    def from_core(step):
        for direction in (0, 1):
            for stage in range(STAGES):
                core_copy(step, direction, stage, 1 - core).wait_recv()

    def part_sem(step, kind):
        return step * CLASSES + kind

    def part_copy(step, kind):
        ref = ygat.at[t, pl.ds(kind * GROUP, GROUP), :]
        return pltpu.make_async_remote_copy(
            src_ref=ref, dst_ref=ref, send_sem=ys.at[part_sem(step, kind)], recv_sem=yr.at[part_sem(step, kind)],
            device_id={"tp": tp_at(step)}, device_id_type=MESH,
        )

    def part_landed(step, kind):
        ref = ygat.at[tp_at(N_TP - step), pl.ds(kind * GROUP, GROUP), :]
        return pltpu.make_async_remote_copy(
            src_ref=ref, dst_ref=ref, send_sem=ys.at[part_sem(step, kind)], recv_sem=yr.at[part_sem(step, kind)],
            device_id={"tp": tp_at(step)}, device_id_type=MESH,
        )

    def pass_on(kind):
        each_of((4 - kind) % 4, lambda step: pooled_landed(step).wait_recv())
        for step in (2, 1, 3):
            part_copy(step, kind).start()

    z_relay(0)
    pooled_sends(0)
    seq_sends(0)
    z_relay(1)
    pooled_sends(3)
    seq_sends(1)
    locals_in[0].start()
    locals_in[1].start()
    z_relay(2)
    pooled_sends(2)
    pooled_sends(1)
    seq_sends(2)
    locals_in[2].start()
    locals_in[3].start()
    x_relay(0)
    pass_on(0)
    z_relay(3)
    seq_sends(3)
    x_relay(1)
    pass_on(1)
    x_relay(2)
    pass_on(2)
    far_relay(0)
    x_relay(3)
    pass_on(3)
    far_relay(1)

    slot = lax.broadcasted_iota(jnp.int32, (SLOTS, SLOTS), 0)
    source = lax.broadcasted_iota(jnp.int32, (SLOTS, SLOTS), 1)
    last = jnp.bitwise_and(source, SLOT - 1) == SLOT - 1
    slot_of = jnp.bitwise_and(distance(jnp.right_shift(slot, 4)) + e, N_ENC - 1)
    source_of = jnp.bitwise_and(distance(jnp.right_shift(source, 4)) + e, N_ENC - 1)
    same = jnp.where((slot_of == source_of) & last, 1.0, 0.0).astype(BF16)
    before = jnp.where((source_of < slot_of) & last, 1.0, 0.0).astype(BF16)
    marks = ygat[t, :, 256:384]
    end_lane = lax.broadcasted_iota(jnp.int32, (SLOTS, 128), 1) == 127
    count = jnp.sum(jnp.where(end_lane, nn(same, marks), 0.0), axis=1, keepdims=True)
    start = jnp.sum(jnp.where(end_lane, nn(before, marks), 0.0), axis=1, keepdims=True)
    first = offset[0].astype(F32)
    end = jnp.max(start + count, axis=0, keepdims=True) + first
    target = lax.broadcasted_iota(jnp.int32, (SLOTS, LANES), 1).astype(F32) - first
    main, spare = slot_maps(start, count, target, 1.0)
    tmap[0] = main
    tmap[1] = spare

    eye = identity(LANES)

    def unpack(step):
        if step:
            for kind in range(CLASSES):
                part_landed(step, kind).wait_recv()
        part = tp_at(N_TP - step)
        rows = decode(ygat[part], tmap[0], tmap[1], eye).astype(BF16)
        for index in range(N_TP):
            place = lax.rem(part * N_TP + index + N_ENC - e, N_ENC)
            chunk = pl.ds(pl.multiple_of(place * CHUNK, CHUNK), CHUNK)
            turned[chunk, :] = rows[index * CHUNK : index * CHUNK + CHUNK]

    unpack(0)
    unpack(1)
    far_relay(2)
    unpack(3)
    unpack(2)
    pooled[...] = nt(eye, turned[...]).astype(BF16)

    sums[...] = jnp.zeros_like(sums)

    def forward(step, which):
        cols = pl.ds(slab_at(step, which), SLAB)
        projected = nn(pooled[0:TOKENS, :], wfull[:, cols]).astype(BF16).astype(F32)
        token = lax.broadcasted_iota(jnp.int32, projected.shape, 0).astype(F32)
        hidden = jnp.where((token >= first) & (token < end), projected, textv[:, cols].astype(F32))
        hid[:, cols] = hidden.astype(BF16)
        squares = hidden * hidden
        slopes = cotv[:, cols].astype(F32) * gain[:, cols] * hidden
        sums[0, 0:TOKENS, :] += squares[:, 0:128] + squares[:, 128:256]
        sums[1, 0:TOKENS, :] += slopes[:, 0:128] + slopes[:, 128:256]

    for copy in locals_in:
        copy.wait()
    forward(0, core)
    forward(1, core)
    forward(3, core)
    far_relay(3)
    for step in (0, 1, 3):
        from_core(step)
        forward(step, 1 - core)
    forward(2, core)
    from_core(2)
    forward(2, 1 - core)

    stats[0] = jnp.zeros((8, LANES), F32)
    stats[0, 0:1, :] = jnp.sum(jnp.transpose(sums[0]), axis=0, keepdims=True)
    stats[0, 1:2, :] = jnp.sum(jnp.transpose(sums[1]), axis=0, keepdims=True)

    def stat_copy(step):
        return pltpu.make_async_remote_copy(
            src_ref=stats.at[0], dst_ref=stats.at[step], send_sem=ss.at[step], recv_sem=sr.at[step],
            device_id={"tp": tp_at(step)}, device_id_type=MESH,
        )

    for step in (2, 1, 3):
        stat_copy(step).start()
    gh[TOKENS:LANES, :] = jnp.zeros((LANES - TOKENS, WIDE), BF16)
    for step in (2, 1, 3):
        stat_copy(step).wait_recv()
    total = (stats[0] + stats[1]) + (stats[2] + stats[3])
    inv_row = lax.rsqrt(total[0:1] / D + EPS)
    slope_row = total[1:2] / D
    inv = column(inv_row, LANES)[0:TOKENS, 0:1]
    back = column(inv_row * inv_row * inv_row * slope_row, LANES)[0:TOKENS, 0:1]

    def backward(index):
        cols = pl.ds(pl.multiple_of(index * SLAB, SLAB), SLAB)
        hidden = hid[:, cols].astype(F32)
        weighted = cotv[:, cols].astype(F32) * gain[:, cols]
        gh[0:TOKENS, cols] = (inv * weighted - back * hidden).astype(BF16)

    def normed(index):
        cols = pl.ds(pl.multiple_of(index * SLAB, SLAB), SLAB)
        mixv[:, cols] = (hid[:, cols].astype(F32) * inv * gain[:, cols]).astype(BF16)

    each(0, WIDE // SLAB, backward)

    def sum_copy(step, kind):
        rows = pl.ds(kind * GROUP, GROUP)
        return pltpu.make_async_remote_copy(
            src_ref=ysend.at[step, rows, :], dst_ref=yrecv.at[step, rows, :],
            send_sem=rs.at[part_sem(step, kind)], recv_sem=rr.at[part_sem(step, kind)],
            device_id={"tp": tp_at(step)}, device_id_type=MESH,
        )

    def back_copy(step):
        return pltpu.make_async_remote_copy(
            src_ref=bsend.at[slot_rows(place_of(step)), :], dst_ref=bret.at[slot_rows(place_of(N_ENC - step)), :],
            send_sem=gs.at[step], recv_sem=gr.at[step], device_id={"enc": enc_at(step)}, device_id_type=MESH,
        )

    def back_landed(step):
        ref = bret.at[slot_rows(place_of(N_ENC - step)), :]
        return pltpu.make_async_remote_copy(
            src_ref=ref, dst_ref=ref, send_sem=gs.at[step], recv_sem=gr.at[step],
            device_id={"enc": enc_at(step)}, device_id_type=MESH,
        )

    main, spare = tmap[0], tmap[1]

    def partial(step):
        places = [lax.rem(tp_at(step) * N_TP + index + N_ENC - e, N_ENC) for index in range(N_TP)]
        chunks = [wfull[pl.ds(pl.multiple_of(place * CHUNK, CHUNK), CHUNK), :] for place in places]
        low, high = encode(main, spare, nt(jnp.concatenate(chunks, axis=0), gh[...]).astype(BF16))
        ysend[step, :, 0:256] = low.astype(BF16)
        ysend[step, :, 256:384] = high.astype(BF16)

    for step in (2, 1, 3):
        partial(step)
        for kind in (0, 1):
            sum_copy(step, kind).start()
    partial(0)
    each(0, WIDE // SLAB, normed)
    mixed_out = pltpu.make_async_copy(mixv, mixed, ls.at[3])
    mixed_out.start()

    for kind in range(CLASSES):
        rows = slice(kind * GROUP, kind * GROUP + GROUP)
        for step in (2, 1, 3):
            sum_copy(step, kind).wait_recv()
            if kind + 2 < CLASSES:
                sum_copy(step, kind + 2).start()
        near = ysend[0, rows, :].astype(F32) + yrecv[1, rows, :].astype(F32)
        far = yrecv[2, rows, :].astype(F32) + yrecv[3, rows, :].astype(F32)
        bsend[rows, :] = (near + far).astype(BF16)
        each_of(kind, lambda step: back_copy(step).start())
    bret[0:SLOT, :] = bsend[0:SLOT, :]

    for direction in (0, 1):
        for stage in range(STAGES):
            for step in (1, 2):
                if reaches(direction, 2 * stage + step):
                    z_copy(direction, 2 * stage, step).wait_send()
            for way in (0, 1):
                x_copy(way, direction, stage).wait_send()
                x_onward(way, direction, stage).wait_send()
            for step in range(N_X):
                core_copy(step, direction, stage, core).wait_send()
    each(1, N_ENC, lambda step: pooled_copy(step).wait_send())
    for step in range(1, N_TP):
        stat_copy(step).wait_send()
        for kind in range(CLASSES):
            part_copy(step, kind).wait_send()

    for step in range(1, N_TP):
        for kind in range(CLASSES):
            sum_copy(step, kind).wait_send()
    each(1, N_ENC, lambda step: back_landed(step).wait_recv())
    grads[...] = decode(bret[...], fmap[0], fmap[1], identity(LANES)).astype(BF16)
    each(1, N_ENC, lambda step: back_copy(step).wait_send())
    mixed_out.wait()


def body(frames, proj_weight, text_emb, norm_gain, cotangent, counts, offsets):
    any_space = pl.BlockSpec(memory_space=pl.ANY)
    vmem = pl.BlockSpec(memory_space=pltpu.VMEM)
    smem = pl.BlockSpec(memory_space=pltpu.SMEM)
    dma = pltpu.SemaphoreType.DMA
    mixed, grads = pl.pallas_call(
        kernel,
        out_shape=(
            jax.ShapeDtypeStruct((TOKENS, WIDE), BF16),
            jax.ShapeDtypeStruct((PART, LANES), BF16),
        ),
        in_specs=[any_space] * 6 + [smem],
        out_specs=(any_space, vmem),
        scratch_shapes=[
            pltpu.VMEM((PART, LANES), BF16),
            pltpu.VMEM((1, WIDE), F32),
            pltpu.VMEM((1, N_ENC), jnp.int32),
            pltpu.VMEM((N_ENC * CHUNK, WIDE), BF16),
            pltpu.VMEM((TOKENS, WIDE), BF16),
            pltpu.VMEM((TOKENS, WIDE), BF16),
            pltpu.VMEM((TOKENS, WIDE), BF16),
            pltpu.VMEM((LANES, WIDE), BF16),
            pltpu.VMEM((TOKENS, WIDE), BF16),
            pltpu.VMEM((N_ENC * CHUNK, LANES), BF16),
            pltpu.VMEM((LANES, N_ENC * CHUNK), BF16),
            pltpu.VMEM((SLOTS, LANES), BF16),
            pltpu.VMEM((N_TP, SLOTS, LANES), BF16),
            pltpu.VMEM((N_TP, SLOTS, LANES), BF16),
            pltpu.VMEM((N_TP, SLOTS, LANES), BF16),
            pltpu.VMEM((N_TP, 8, LANES), F32),
            pltpu.VMEM((2, LANES, 128), F32),
            pltpu.VMEM((SLOTS, LANES), BF16),
            pltpu.VMEM((SLOTS, LANES), BF16),
            pltpu.VMEM((2, SLOTS, LANES), BF16),
            pltpu.VMEM((2, SLOTS, LANES), BF16),
            *[dma((4 * STAGES,)) for _ in range(6)],
            *[dma((8 * STAGES,)) for _ in range(2)],
            *[dma((N_ENC,)) for _ in range(2)],
            *[dma((N_TP * CLASSES,)) for _ in range(2)],
            *[dma((N_TP,)) for _ in range(2)],
            *[dma((N_TP * CLASSES,)) for _ in range(2)],
            *[dma((N_ENC,)) for _ in range(2)],
            dma((7,)),
        ],
        compiler_params=pltpu.CompilerParams(
            collective_id=0, has_side_effects=True, vmem_limit_bytes=56 * 1024 * 1024
        ),
    )(frames.T, proj_weight, text_emb, norm_gain.reshape(1, WIDE), cotangent, counts, offsets)
    return mixed, grads.T


def solution(mesh):
    in_specs = (
        P(("enc", "seq"), "tp"),
        P("enc", "tp"),
        P(("enc", "seq"), "tp"),
        P("tp"),
        P(("enc", "seq"), "tp"),
        P(("enc", "seq"), None),
        P(("enc", "seq")),
    )
    out_specs = (P(("enc", "seq"), "tp"), P(("enc", "seq"), "tp"))
    return jax.shard_map(body, mesh=mesh, in_specs=in_specs, out_specs=out_specs, check_vma=False)
```

```python
import jax
import jax.numpy as jnp
from jax import lax
from jax.experimental import pallas as pl
from jax.experimental.pallas import tpu as pltpu
from jax.sharding import PartitionSpec as P

D = 8192
EPS = 1e-05
MESH = pl.DeviceIdType.MESH
F32 = jnp.float32
BF16 = jnp.bfloat16

N_ENC = 16
N_X = 4
N_TP = 4
CHUNK = 80
WIDE = 2048
PART = 320
SLAB = 256
HALF = 128
SLOT = 16
SLOTS = N_ENC * SLOT
LANES = 384
TOKENS = 320
STAGES = 4
CLASSES = 4
GROUP = SLOTS // CLASSES


def nt(a, b):
    return lax.dot_general(a, b, (((1,), (1,)), ((), ())), preferred_element_type=F32)


def nn(a, b):
    return jnp.dot(a, b, preferred_element_type=F32)


def identity(size):
    rows = lax.broadcasted_iota(jnp.int32, (size, size), 0)
    cols = lax.broadcasted_iota(jnp.int32, (size, size), 1)
    return (rows == cols).astype(F32).astype(BF16)


def slot_maps(start, count, target, value):
    place = jnp.bitwise_and(lax.broadcasted_iota(jnp.int32, target.shape, 0), SLOT - 1)
    placef = place.astype(F32)
    main = (start + placef == target) & (placef < count)
    extra = jnp.where(place >= 5, 17.0, 16.0)
    spare = (start + extra == target) & (extra < count) & (place < 10)
    zero = jnp.zeros_like(target)
    return jnp.where(main, value, zero).astype(BF16), jnp.where(spare, value, zero).astype(BF16)


def piece_mask(shape, axis, piece):
    place = jnp.bitwise_and(lax.broadcasted_iota(jnp.int32, shape, axis), SLOT - 1)
    return (place == piece) | (place == piece + 5)


def distance(place):
    return jnp.bitwise_and(place, 3) * 4 + jnp.right_shift(place, 2)


def encode(main, spare, items):
    low = nt(main, items[0:256])
    none = jnp.zeros((64, items.shape[1]), BF16)
    high = nt(main, jnp.concatenate([items[256:320], none], axis=0))
    for piece in range(5):
        part = nt(spare, jnp.concatenate([none, items[64 * piece : 64 * piece + 64]], axis=0))
        high = high + jnp.where(piece_mask(part.shape, 0, piece), part, 0.0)
    return low, high


def decode(slots, main, spare, eye):
    turned = nt(eye, slots)
    rest = turned[320:384]
    pieces = [jnp.where(piece_mask(rest.shape, 1, piece), rest, 0.0) for piece in range(5)]
    stacked = jnp.concatenate(pieces, axis=0).astype(BF16)
    return nn(turned[0:320].astype(BF16), main) + nn(stacked, spare)


def column(row, size):
    return jnp.transpose(jnp.broadcast_to(row, (128, size)))


def kernel(
    frames_in, weight, text, gain_in, cot, counts_in, offset, mixed, grads,
    frames, gain, counts, wfull, textv, cotv, hid, gh, mixv, turned, pooled, slots, ygat, ysend, yrecv, stats, sums, bsend, bret, fmap, tmap,
    zs, zr, xs, xr, us, ur, cs, cr, fs, fr, ys, yr, ss, sr, rs, rr, gs, gr, ls,
):
    e, s, t = lax.axis_index("enc"), lax.axis_index("seq"), lax.axis_index("tp")
    core = lax.rem(s, 2)
    chip = lax.div(s, 2)
    other = s + 1 - 2 * core
    x_next = lax.rem(chip + 1, N_X) * 2 + core
    x_prev = lax.rem(chip + N_X - 1, N_X) * 2 + core

    def slab_at(step, which):
        return pl.multiple_of((lax.rem(chip + step, N_X) * 2 + which) * SLAB, SLAB)

    def enc_at(step):
        return lax.rem(e + step + 2 * N_ENC, N_ENC)

    def tp_at(step):
        return lax.rem(t + step, N_TP)

    barrier = pltpu.get_barrier_semaphore()

    def greet(step, carry):
        pl.semaphore_signal(barrier, inc=1, device_id={"enc": enc_at(step)}, device_id_type=MESH)
        return carry

    lax.fori_loop(1, N_ENC, greet, 0)
    for step in range(1, N_TP):
        pl.semaphore_signal(barrier, inc=1, device_id={"tp": tp_at(step)}, device_id_type=MESH)
    for peer in (other, x_next, x_prev):
        pl.semaphore_signal(barrier, inc=1, device_id={"seq": peer}, device_id_type=MESH)

    locals_in = [
        pltpu.make_async_copy(weight, wfull.at[0:CHUNK, :], ls.at[0]),
        pltpu.make_async_copy(text, textv, ls.at[1]),
        pltpu.make_async_copy(cot, cotv, ls.at[2]),
        pltpu.make_async_copy(gain_in, gain, ls.at[6]),
    ]
    first_in = [
        pltpu.make_async_copy(counts_in, counts, ls.at[4]),
        pltpu.make_async_copy(frames_in, frames, ls.at[5]),
    ]
    for copy in first_in:
        copy.start()

    pl.semaphore_wait(barrier, N_ENC - 1 + N_TP - 1 + 3)

    def chunk_rows(direction, far):
        return pl.ds(((N_ENC - far) if direction == 0 else far) * CHUNK, CHUNK)

    my_cols = pl.ds(slab_at(0, core), SLAB)

    def z_copy(direction, base, step):
        src = wfull.at[chunk_rows(direction, base), my_cols] if base else weight.at[:, my_cols]
        index = direction * 8 + base + step - 1
        return pltpu.make_async_remote_copy(
            src_ref=src, dst_ref=wfull.at[chunk_rows(direction, base + step), my_cols],
            send_sem=zs.at[index], recv_sem=zr.at[index],
            device_id={"enc": enc_at(step if direction == 0 else -step)}, device_id_type=MESH,
        )

    def reaches(direction, far):
        return far <= (8 if direction == 0 else 7)

    def z_sends(direction, base):
        for step in (2, 1):
            if reaches(direction, base + step):
                z_copy(direction, base, step).start()

    def z_landed(direction, far):
        step = 2 if far % 2 == 0 else 1
        z_copy(direction, far - step, step).wait_recv()

    def group_rows(direction, stage):
        if direction == 0:
            return pl.ds((N_ENC - 2 - 2 * stage) * CHUNK, 2 * CHUNK)
        return pl.ds((2 * stage + 1) * CHUNK, (2 if stage < STAGES - 1 else 1) * CHUNK)

    def seq_copy(ref, send, recv, index, to):
        return pltpu.make_async_remote_copy(
            src_ref=ref, dst_ref=ref, send_sem=send.at[index], recv_sem=recv.at[index],
            device_id={"seq": to}, device_id_type=MESH,
        )

    def x_copy(way, direction, stage):
        index = (way * 2 + direction) * STAGES + stage
        ref = wfull.at[group_rows(direction, stage), my_cols]
        return seq_copy(ref, xs, xr, index, x_next if way == 0 else x_prev)

    def x_landed(way, direction, stage):
        index = (way * 2 + direction) * STAGES + stage
        ref = wfull.at[group_rows(direction, stage), pl.ds(slab_at(3 if way == 0 else 1, core), SLAB)]
        seq_copy(ref, xs, xr, index, x_next if way == 0 else x_prev).wait_recv()

    def x_onward(way, direction, stage):
        index = (way * 2 + direction) * STAGES + stage
        cols = pl.ds(pl.multiple_of(slab_at(3 if way == 0 else 1, core) + way * HALF, HALF), HALF)
        return seq_copy(wfull.at[group_rows(direction, stage), cols], us, ur, index, x_next if way == 0 else x_prev)

    def far_landed(way, direction, stage):
        index = (way * 2 + direction) * STAGES + stage
        cols = pl.ds(pl.multiple_of(slab_at(2, core) + way * HALF, HALF), HALF)
        ref = wfull.at[group_rows(direction, stage), cols]
        seq_copy(ref, us, ur, index, x_next if way == 0 else x_prev).wait_recv()

    def core_copy(step, direction, stage, which):
        index = (step * 2 + direction) * STAGES + stage
        ref = wfull.at[group_rows(direction, stage), pl.ds(slab_at(step, which), SLAB)]
        return seq_copy(ref, cs, cr, index, other)

    def slot_rows(place):
        return pl.ds(pl.multiple_of(place * SLOT, SLOT), SLOT)

    def place_of(step):
        return lax.rem(step, 4) * 4 + lax.div(step, 4)

    def class_steps(kind):
        return (1 if kind == 0 else 0, 4), lambda index: 4 * index + kind

    def pooled_copy(step):
        return pltpu.make_async_remote_copy(
            src_ref=slots.at[slot_rows(place_of(step)), :],
            dst_ref=ygat.at[t, slot_rows(place_of(N_ENC - step)), :],
            send_sem=fs.at[step], recv_sem=fr.at[step], device_id={"enc": enc_at(step)}, device_id_type=MESH,
        )

    def pooled_landed(step):
        ref = ygat.at[t, slot_rows(place_of(N_ENC - step)), :]
        return pltpu.make_async_remote_copy(
            src_ref=ref, dst_ref=ref, send_sem=fs.at[step], recv_sem=fr.at[step],
            device_id={"enc": enc_at(step)}, device_id_type=MESH,
        )

    def each(low_step, high_step, do):
        def body(step, carry):
            do(step)
            return carry

        lax.fori_loop(low_step, high_step, body, 0)

    def each_of(kind, do):
        (low_index, high_index), step_of = class_steps(kind)
        each(low_index, high_index, lambda index: do(step_of(index)))

    for direction in (0, 1):
        z_sends(direction, 0)

    for copy in first_in:
        copy.wait()
    row = lax.broadcasted_iota(jnp.int32, (SLOTS, N_ENC), 0)
    lane = lax.broadcasted_iota(jnp.int32, (SLOTS, N_ENC), 1)
    dealt = jnp.broadcast_to(counts[...].astype(F32), (SLOTS, N_ENC))
    block = jnp.bitwise_and(distance(jnp.right_shift(row, 4)) + e, N_ENC - 1)
    count = jnp.sum(jnp.where(lane == block, dealt, 0.0), axis=1, keepdims=True)
    start = jnp.sum(jnp.where(lane < block, dealt, 0.0), axis=1, keepdims=True)
    target = jnp.right_shift(lax.broadcasted_iota(jnp.int32, (SLOTS, LANES), 1), 1).astype(F32)
    main, spare = slot_maps(start, count, target, 0.5)
    fmap[0] = main
    fmap[1] = spare
    low, high = encode(main, spare, frames[...])
    place = jnp.bitwise_and(lax.broadcasted_iota(jnp.int32, high.shape, 0), SLOT - 1)
    in_spare = lax.broadcasted_iota(jnp.int32, high.shape, 1) >= 64
    high = jnp.where((place >= 10) & in_spare, count, high)
    slots[:, 0:256] = low.astype(BF16)
    slots[:, 256:384] = high.astype(BF16)
    ygat[t, 0:SLOT, :] = slots[0:SLOT, :]

    def z_relay(stage):
        for direction in (0, 1):
            if reaches(direction, 2 * stage + 2):
                z_landed(direction, 2 * stage + 2)
                z_sends(direction, 2 * stage + 2)

    def seq_sends(stage):
        for direction in (0, 1):
            z_landed(direction, 2 * stage + 1)
            for way in (0, 1):
                x_copy(way, direction, stage).start()
            core_copy(0, direction, stage, core).start()

    def pooled_sends(kind):
        each_of(kind, lambda step: pooled_copy(step).start())

    def x_relay(stage):
        for direction in (0, 1):
            for way in (0, 1):
                x_landed(way, direction, stage)
                x_onward(way, direction, stage).start()
                core_copy(3 if way == 0 else 1, direction, stage, core).start()

    def far_relay(stage):
        for direction in (0, 1):
            for way in (0, 1):
                far_landed(way, direction, stage)
            core_copy(2, direction, stage, core).start()

    def from_core(step):
        for direction in (0, 1):
            for stage in range(STAGES):
                core_copy(step, direction, stage, 1 - core).wait_recv()

    def part_sem(step, kind):
        return step * CLASSES + kind

    def part_copy(step, kind):
        ref = ygat.at[t, pl.ds(kind * GROUP, GROUP), :]
        return pltpu.make_async_remote_copy(
            src_ref=ref, dst_ref=ref, send_sem=ys.at[part_sem(step, kind)], recv_sem=yr.at[part_sem(step, kind)],
            device_id={"tp": tp_at(step)}, device_id_type=MESH,
        )

    def part_landed(step, kind):
        ref = ygat.at[tp_at(N_TP - step), pl.ds(kind * GROUP, GROUP), :]
        return pltpu.make_async_remote_copy(
            src_ref=ref, dst_ref=ref, send_sem=ys.at[part_sem(step, kind)], recv_sem=yr.at[part_sem(step, kind)],
            device_id={"tp": tp_at(step)}, device_id_type=MESH,
        )

    def pass_on(kind):
        each_of((4 - kind) % 4, lambda step: pooled_landed(step).wait_recv())
        for step in (2, 1, 3):
            part_copy(step, kind).start()

    pooled_sends(0)
    z_relay(0)
    pooled_sends(3)
    seq_sends(0)
    z_relay(1)
    pooled_sends(2)
    pooled_sends(1)
    seq_sends(1)
    locals_in[0].start()
    locals_in[1].start()
    z_relay(2)
    seq_sends(2)
    locals_in[2].start()
    locals_in[3].start()
    x_relay(0)
    pass_on(0)
    pass_on(1)
    z_relay(3)
    seq_sends(3)
    pass_on(2)
    x_relay(1)
    pass_on(3)
    x_relay(2)
    far_relay(0)

    slot = lax.broadcasted_iota(jnp.int32, (SLOTS, SLOTS), 0)
    source = lax.broadcasted_iota(jnp.int32, (SLOTS, SLOTS), 1)
    last = jnp.bitwise_and(source, SLOT - 1) == SLOT - 1
    slot_of = jnp.bitwise_and(distance(jnp.right_shift(slot, 4)) + e, N_ENC - 1)
    source_of = jnp.bitwise_and(distance(jnp.right_shift(source, 4)) + e, N_ENC - 1)
    same = jnp.where((slot_of == source_of) & last, 1.0, 0.0).astype(BF16)
    before = jnp.where((source_of < slot_of) & last, 1.0, 0.0).astype(BF16)
    marks = ygat[t, :, 256:384]
    end_lane = lax.broadcasted_iota(jnp.int32, (SLOTS, 128), 1) == 127
    count = jnp.sum(jnp.where(end_lane, nn(same, marks), 0.0), axis=1, keepdims=True)
    start = jnp.sum(jnp.where(end_lane, nn(before, marks), 0.0), axis=1, keepdims=True)
    first = offset[0].astype(F32)
    end = jnp.max(start + count, axis=0, keepdims=True) + first
    target = lax.broadcasted_iota(jnp.int32, (SLOTS, LANES), 1).astype(F32) - first
    main, spare = slot_maps(start, count, target, 1.0)
    tmap[0] = main
    tmap[1] = spare

    x_relay(3)
    far_relay(1)

    eye = identity(LANES)

    def unpack(step):
        if step:
            for kind in range(CLASSES):
                part_landed(step, kind).wait_recv()
        part = tp_at(N_TP - step)
        rows = decode(ygat[part], tmap[0], tmap[1], eye).astype(BF16)
        for index in range(N_TP):
            place = lax.rem(part * N_TP + index + N_ENC - e, N_ENC)
            chunk = pl.ds(pl.multiple_of(place * CHUNK, CHUNK), CHUNK)
            turned[chunk, :] = rows[index * CHUNK : index * CHUNK + CHUNK]

    unpack(0)
    unpack(1)
    far_relay(2)
    unpack(3)
    unpack(2)
    pooled[...] = nt(eye, turned[...]).astype(BF16)

    sums[...] = jnp.zeros_like(sums)

    def forward(step, which):
        cols = pl.ds(slab_at(step, which), SLAB)
        projected = nn(pooled[0:TOKENS, :], wfull[:, cols]).astype(BF16).astype(F32)
        token = lax.broadcasted_iota(jnp.int32, projected.shape, 0).astype(F32)
        hidden = jnp.where((token >= first) & (token < end), projected, textv[:, cols].astype(F32))
        hid[:, cols] = hidden.astype(BF16)
        squares = hidden * hidden
        slopes = cotv[:, cols].astype(F32) * gain[:, cols] * hidden
        sums[0, 0:TOKENS, :] += squares[:, 0:128] + squares[:, 128:256]
        sums[1, 0:TOKENS, :] += slopes[:, 0:128] + slopes[:, 128:256]

    for copy in locals_in:
        copy.wait()
    forward(0, core)
    far_relay(3)
    forward(1, core)
    forward(3, core)
    for step in (0, 1, 3):
        from_core(step)
        forward(step, 1 - core)
    forward(2, core)
    from_core(2)
    forward(2, 1 - core)

    stats[0] = jnp.zeros((8, LANES), F32)
    stats[0, 0:1, :] = jnp.sum(jnp.transpose(sums[0]), axis=0, keepdims=True)
    stats[0, 1:2, :] = jnp.sum(jnp.transpose(sums[1]), axis=0, keepdims=True)

    def stat_copy(step):
        return pltpu.make_async_remote_copy(
            src_ref=stats.at[0], dst_ref=stats.at[step], send_sem=ss.at[step], recv_sem=sr.at[step],
            device_id={"tp": tp_at(step)}, device_id_type=MESH,
        )

    for step in (2, 1, 3):
        stat_copy(step).start()
    gh[TOKENS:LANES, :] = jnp.zeros((LANES - TOKENS, WIDE), BF16)
    for direction in (0, 1):
        for stage in range(STAGES):
            for step in (1, 2):
                if reaches(direction, 2 * stage + step):
                    z_copy(direction, 2 * stage, step).wait_send()
            for way in (0, 1):
                x_copy(way, direction, stage).wait_send()
                x_onward(way, direction, stage).wait_send()
            for step in range(N_X):
                core_copy(step, direction, stage, core).wait_send()

    for step in (2, 1, 3):
        stat_copy(step).wait_recv()
    total = (stats[0] + stats[1]) + (stats[2] + stats[3])
    inv_row = lax.rsqrt(total[0:1] / D + EPS)
    slope_row = total[1:2] / D
    inv = column(inv_row, LANES)[0:TOKENS]
    back = column(inv_row * inv_row * inv_row * slope_row, LANES)[0:TOKENS]
    inv = jnp.concatenate([inv, inv], axis=1)
    back = jnp.concatenate([back, back], axis=1)

    def backward(index):
        cols = pl.ds(pl.multiple_of(index * SLAB, SLAB), SLAB)
        hidden = hid[:, cols].astype(F32)
        weighted = cotv[:, cols].astype(F32) * gain[:, cols]
        gh[0:TOKENS, cols] = (inv * weighted - back * hidden).astype(BF16)

    def normed(index):
        cols = pl.ds(pl.multiple_of(index * SLAB, SLAB), SLAB)
        mixv[:, cols] = (hid[:, cols].astype(F32) * inv * gain[:, cols]).astype(BF16)

    each(0, WIDE // SLAB, backward)

    def sum_copy(step, kind):
        rows = pl.ds(kind * GROUP, GROUP)
        return pltpu.make_async_remote_copy(
            src_ref=ysend.at[step, rows, :], dst_ref=yrecv.at[step, rows, :],
            send_sem=rs.at[part_sem(step, kind)], recv_sem=rr.at[part_sem(step, kind)],
            device_id={"tp": tp_at(step)}, device_id_type=MESH,
        )

    def back_copy(step):
        return pltpu.make_async_remote_copy(
            src_ref=bsend.at[slot_rows(place_of(step)), :], dst_ref=bret.at[slot_rows(place_of(N_ENC - step)), :],
            send_sem=gs.at[step], recv_sem=gr.at[step], device_id={"enc": enc_at(step)}, device_id_type=MESH,
        )

    def back_landed(step):
        ref = bret.at[slot_rows(place_of(N_ENC - step)), :]
        return pltpu.make_async_remote_copy(
            src_ref=ref, dst_ref=ref, send_sem=gs.at[step], recv_sem=gr.at[step],
            device_id={"enc": enc_at(step)}, device_id_type=MESH,
        )

    main, spare = tmap[0], tmap[1]

    def partial(step):
        places = [lax.rem(tp_at(step) * N_TP + index + N_ENC - e, N_ENC) for index in range(N_TP)]
        chunks = [wfull[pl.ds(pl.multiple_of(place * CHUNK, CHUNK), CHUNK), :] for place in places]
        low, high = encode(main, spare, nt(jnp.concatenate(chunks, axis=0), gh[...]).astype(BF16))
        ysend[step, :, 0:256] = low.astype(BF16)
        ysend[step, :, 256:384] = high.astype(BF16)

    for step in (2, 1, 3):
        partial(step)
        for kind in (0, 1):
            sum_copy(step, kind).start()
    partial(0)
    for step in (2, 1, 3):
        sum_copy(step, 2).start()
    each(0, WIDE // SLAB, normed)
    for step in (2, 1, 3):
        sum_copy(step, 3).start()
    mixed_out = pltpu.make_async_copy(mixv, mixed, ls.at[3])
    mixed_out.start()

    for kind in range(CLASSES):
        rows = slice(kind * GROUP, kind * GROUP + GROUP)
        for step in (2, 1, 3):
            sum_copy(step, kind).wait_recv()
        near = ysend[0, rows, :].astype(F32) + yrecv[1, rows, :].astype(F32)
        far = yrecv[2, rows, :].astype(F32) + yrecv[3, rows, :].astype(F32)
        bsend[rows, :] = (near + far).astype(BF16)
        each_of(kind, lambda step: back_copy(step).start())
    bret[0:SLOT, :] = bsend[0:SLOT, :]

    each(1, N_ENC, lambda step: pooled_copy(step).wait_send())
    for step in range(1, N_TP):
        stat_copy(step).wait_send()
        for kind in range(CLASSES):
            part_copy(step, kind).wait_send()

    for step in range(1, N_TP):
        for kind in range(CLASSES):
            sum_copy(step, kind).wait_send()
    each(1, N_ENC, lambda step: back_landed(step).wait_recv())
    grads[...] = decode(bret[...], fmap[0], fmap[1], identity(LANES)).astype(BF16)
    each(1, N_ENC, lambda step: back_copy(step).wait_send())
    mixed_out.wait()


def body(frames, proj_weight, text_emb, norm_gain, cotangent, counts, offsets):
    any_space = pl.BlockSpec(memory_space=pl.ANY)
    vmem = pl.BlockSpec(memory_space=pltpu.VMEM)
    smem = pl.BlockSpec(memory_space=pltpu.SMEM)
    dma = pltpu.SemaphoreType.DMA
    mixed, grads = pl.pallas_call(
        kernel,
        out_shape=(
            jax.ShapeDtypeStruct((TOKENS, WIDE), BF16),
            jax.ShapeDtypeStruct((PART, LANES), BF16),
        ),
        in_specs=[any_space] * 6 + [smem],
        out_specs=(any_space, vmem),
        scratch_shapes=[
            pltpu.VMEM((PART, LANES), BF16),
            pltpu.VMEM((1, WIDE), F32),
            pltpu.VMEM((1, N_ENC), jnp.int32),
            pltpu.VMEM((N_ENC * CHUNK, WIDE), BF16),
            pltpu.VMEM((TOKENS, WIDE), BF16),
            pltpu.VMEM((TOKENS, WIDE), BF16),
            pltpu.VMEM((TOKENS, WIDE), BF16),
            pltpu.VMEM((LANES, WIDE), BF16),
            pltpu.VMEM((TOKENS, WIDE), BF16),
            pltpu.VMEM((N_ENC * CHUNK, LANES), BF16),
            pltpu.VMEM((LANES, N_ENC * CHUNK), BF16),
            pltpu.VMEM((SLOTS, LANES), BF16),
            pltpu.VMEM((N_TP, SLOTS, LANES), BF16),
            pltpu.VMEM((N_TP, SLOTS, LANES), BF16),
            pltpu.VMEM((N_TP, SLOTS, LANES), BF16),
            pltpu.VMEM((N_TP, 8, LANES), F32),
            pltpu.VMEM((2, LANES, 128), F32),
            pltpu.VMEM((SLOTS, LANES), BF16),
            pltpu.VMEM((SLOTS, LANES), BF16),
            pltpu.VMEM((2, SLOTS, LANES), BF16),
            pltpu.VMEM((2, SLOTS, LANES), BF16),
            *[dma((4 * STAGES,)) for _ in range(6)],
            *[dma((8 * STAGES,)) for _ in range(2)],
            *[dma((N_ENC,)) for _ in range(2)],
            *[dma((N_TP * CLASSES,)) for _ in range(2)],
            *[dma((N_TP,)) for _ in range(2)],
            *[dma((N_TP * CLASSES,)) for _ in range(2)],
            *[dma((N_ENC,)) for _ in range(2)],
            dma((7,)),
        ],
        compiler_params=pltpu.CompilerParams(
            collective_id=0, has_side_effects=True, vmem_limit_bytes=56 * 1024 * 1024
        ),
    )(frames.T, proj_weight, text_emb, norm_gain.reshape(1, WIDE), cotangent, counts, offsets)
    return mixed, grads.T


def solution(mesh):
    in_specs = (
        P(("enc", "seq"), "tp"),
        P("enc", "tp"),
        P(("enc", "seq"), "tp"),
        P("tp"),
        P(("enc", "seq"), "tp"),
        P(("enc", "seq"), None),
        P(("enc", "seq")),
    )
    out_specs = (P(("enc", "seq"), "tp"), P(("enc", "seq"), "tp"))
    return jax.shard_map(body, mesh=mesh, in_specs=in_specs, out_specs=out_specs, check_vma=False)
```

```python
import jax
import jax.numpy as jnp
from jax import lax
from jax.experimental import pallas as pl
from jax.experimental.pallas import tpu as pltpu
from jax.sharding import PartitionSpec as P

D = 8192
EPS = 1e-05
MESH = pl.DeviceIdType.MESH
F32 = jnp.float32
BF16 = jnp.bfloat16

N_ENC = 16
N_X = 4
N_TP = 4
CHUNK = 80
WIDE = 2048
PART = 320
SLAB = 256
HALF = 128
SLOT = 16
SLOTS = N_ENC * SLOT
LANES = 384
TOKENS = 320
STAGES = 4
CLASSES = 4
GROUP = SLOTS // CLASSES


def nt(a, b):
    return lax.dot_general(a, b, (((1,), (1,)), ((), ())), preferred_element_type=F32)


def nn(a, b):
    return jnp.dot(a, b, preferred_element_type=F32)


def identity(size):
    rows = lax.broadcasted_iota(jnp.int32, (size, size), 0)
    cols = lax.broadcasted_iota(jnp.int32, (size, size), 1)
    return (rows == cols).astype(F32).astype(BF16)


def slot_maps(start, count, target, value):
    place = jnp.bitwise_and(lax.broadcasted_iota(jnp.int32, target.shape, 0), SLOT - 1)
    placef = place.astype(F32)
    main = (start + placef == target) & (placef < count)
    extra = jnp.where(place >= 5, 17.0, 16.0)
    spare = (start + extra == target) & (extra < count) & (place < 10)
    zero = jnp.zeros_like(target)
    return jnp.where(main, value, zero).astype(BF16), jnp.where(spare, value, zero).astype(BF16)


def piece_mask(shape, axis, piece):
    place = jnp.bitwise_and(lax.broadcasted_iota(jnp.int32, shape, axis), SLOT - 1)
    return (place == piece) | (place == piece + 5)


def distance(place):
    return jnp.bitwise_and(place, 3) * 4 + jnp.right_shift(place, 2)


def encode(main, spare, items):
    low = nt(main, items[0:256])
    none = jnp.zeros((64, items.shape[1]), BF16)
    high = nt(main, jnp.concatenate([items[256:320], none], axis=0))
    for piece in range(5):
        part = nt(spare, jnp.concatenate([none, items[64 * piece : 64 * piece + 64]], axis=0))
        high = high + jnp.where(piece_mask(part.shape, 0, piece), part, 0.0)
    return low, high


def decode(slots, main, spare, eye):
    turned = nt(eye, slots)
    rest = turned[320:384]
    pieces = [jnp.where(piece_mask(rest.shape, 1, piece), rest, 0.0) for piece in range(5)]
    stacked = jnp.concatenate(pieces, axis=0).astype(BF16)
    return nn(turned[0:320].astype(BF16), main) + nn(stacked, spare)


def column(row, size):
    return jnp.transpose(jnp.broadcast_to(row, (128, size)))


def kernel(
    frames_in, weight, text, gain_in, cot, counts_in, offset, mixed, grads,
    frames, gain, counts, wfull, textv, cotv, hid, gh, mixv, turned, pooled, slots, ygat, ysend, yrecv, stats, sums, bsend, bret, fmap, tmap,
    zs, zr, xs, xr, us, ur, cs, cr, fs, fr, ys, yr, ss, sr, rs, rr, gs, gr, ls,
):
    e, s, t = lax.axis_index("enc"), lax.axis_index("seq"), lax.axis_index("tp")
    core = lax.rem(s, 2)
    chip = lax.div(s, 2)
    other = s + 1 - 2 * core
    x_next = lax.rem(chip + 1, N_X) * 2 + core
    x_prev = lax.rem(chip + N_X - 1, N_X) * 2 + core

    def slab_at(step, which):
        return pl.multiple_of((lax.rem(chip + step, N_X) * 2 + which) * SLAB, SLAB)

    def enc_at(step):
        return lax.rem(e + step + 2 * N_ENC, N_ENC)

    def tp_at(step):
        return lax.rem(t + step, N_TP)

    barrier = pltpu.get_barrier_semaphore()

    def greet(step, carry):
        pl.semaphore_signal(barrier, inc=1, device_id={"enc": enc_at(step)}, device_id_type=MESH)
        return carry

    lax.fori_loop(1, N_ENC, greet, 0)
    for step in range(1, N_TP):
        pl.semaphore_signal(barrier, inc=1, device_id={"tp": tp_at(step)}, device_id_type=MESH)
    for peer in (other, x_next, x_prev):
        pl.semaphore_signal(barrier, inc=1, device_id={"seq": peer}, device_id_type=MESH)

    locals_in = [
        pltpu.make_async_copy(weight, wfull.at[0:CHUNK, :], ls.at[0]),
        pltpu.make_async_copy(text, textv, ls.at[1]),
        pltpu.make_async_copy(cot, cotv, ls.at[2]),
        pltpu.make_async_copy(gain_in, gain, ls.at[6]),
    ]
    first_in = [
        pltpu.make_async_copy(counts_in, counts, ls.at[4]),
        pltpu.make_async_copy(frames_in, frames, ls.at[5]),
    ]
    for copy in first_in:
        copy.start()

    pl.semaphore_wait(barrier, N_ENC - 1 + N_TP - 1 + 3)

    def chunk_rows(direction, far):
        return pl.ds(((N_ENC - far) if direction == 0 else far) * CHUNK, CHUNK)

    my_cols = pl.ds(slab_at(0, core), SLAB)

    def z_copy(direction, base, step):
        src = wfull.at[chunk_rows(direction, base), my_cols] if base else weight.at[:, my_cols]
        index = direction * 8 + base + step - 1
        return pltpu.make_async_remote_copy(
            src_ref=src, dst_ref=wfull.at[chunk_rows(direction, base + step), my_cols],
            send_sem=zs.at[index], recv_sem=zr.at[index],
            device_id={"enc": enc_at(step if direction == 0 else -step)}, device_id_type=MESH,
        )

    def reaches(direction, far):
        return far <= (8 if direction == 0 else 7)

    def z_sends(direction, base):
        for step in (2, 1):
            if reaches(direction, base + step):
                z_copy(direction, base, step).start()

    def z_landed(direction, far):
        step = 2 if far % 2 == 0 else 1
        z_copy(direction, far - step, step).wait_recv()

    def group_rows(direction, stage):
        if direction == 0:
            return pl.ds((N_ENC - 2 - 2 * stage) * CHUNK, 2 * CHUNK)
        return pl.ds((2 * stage + 1) * CHUNK, (2 if stage < STAGES - 1 else 1) * CHUNK)

    def seq_copy(ref, send, recv, index, to):
        return pltpu.make_async_remote_copy(
            src_ref=ref, dst_ref=ref, send_sem=send.at[index], recv_sem=recv.at[index],
            device_id={"seq": to}, device_id_type=MESH,
        )

    def x_copy(way, direction, stage):
        index = (way * 2 + direction) * STAGES + stage
        ref = wfull.at[group_rows(direction, stage), my_cols]
        return seq_copy(ref, xs, xr, index, x_next if way == 0 else x_prev)

    def x_landed(way, direction, stage):
        index = (way * 2 + direction) * STAGES + stage
        ref = wfull.at[group_rows(direction, stage), pl.ds(slab_at(3 if way == 0 else 1, core), SLAB)]
        seq_copy(ref, xs, xr, index, x_next if way == 0 else x_prev).wait_recv()

    def x_onward(way, direction, stage):
        index = (way * 2 + direction) * STAGES + stage
        cols = pl.ds(pl.multiple_of(slab_at(3 if way == 0 else 1, core) + way * HALF, HALF), HALF)
        return seq_copy(wfull.at[group_rows(direction, stage), cols], us, ur, index, x_next if way == 0 else x_prev)

    def far_landed(way, direction, stage):
        index = (way * 2 + direction) * STAGES + stage
        cols = pl.ds(pl.multiple_of(slab_at(2, core) + way * HALF, HALF), HALF)
        ref = wfull.at[group_rows(direction, stage), cols]
        seq_copy(ref, us, ur, index, x_next if way == 0 else x_prev).wait_recv()

    def core_copy(step, direction, stage, which):
        index = (step * 2 + direction) * STAGES + stage
        ref = wfull.at[group_rows(direction, stage), pl.ds(slab_at(step, which), SLAB)]
        return seq_copy(ref, cs, cr, index, other)

    def slot_rows(place):
        return pl.ds(pl.multiple_of(place * SLOT, SLOT), SLOT)

    def place_of(step):
        return lax.rem(step, 4) * 4 + lax.div(step, 4)

    def class_steps(kind):
        return (1 if kind == 0 else 0, 4), lambda index: 4 * index + kind

    def pooled_copy(step):
        return pltpu.make_async_remote_copy(
            src_ref=slots.at[slot_rows(place_of(step)), :],
            dst_ref=ygat.at[t, slot_rows(place_of(N_ENC - step)), :],
            send_sem=fs.at[step], recv_sem=fr.at[step], device_id={"enc": enc_at(step)}, device_id_type=MESH,
        )

    def pooled_landed(step):
        ref = ygat.at[t, slot_rows(place_of(N_ENC - step)), :]
        return pltpu.make_async_remote_copy(
            src_ref=ref, dst_ref=ref, send_sem=fs.at[step], recv_sem=fr.at[step],
            device_id={"enc": enc_at(step)}, device_id_type=MESH,
        )

    def each(low_step, high_step, do):
        def body(step, carry):
            do(step)
            return carry

        lax.fori_loop(low_step, high_step, body, 0)

    def each_of(kind, do):
        (low_index, high_index), step_of = class_steps(kind)
        each(low_index, high_index, lambda index: do(step_of(index)))

    for direction in (0, 1):
        z_sends(direction, 0)

    for copy in first_in:
        copy.wait()
    row = lax.broadcasted_iota(jnp.int32, (SLOTS, N_ENC), 0)
    lane = lax.broadcasted_iota(jnp.int32, (SLOTS, N_ENC), 1)
    dealt = jnp.broadcast_to(counts[...].astype(F32), (SLOTS, N_ENC))
    block = jnp.bitwise_and(distance(jnp.right_shift(row, 4)) + e, N_ENC - 1)
    count = jnp.sum(jnp.where(lane == block, dealt, 0.0), axis=1, keepdims=True)
    start = jnp.sum(jnp.where(lane < block, dealt, 0.0), axis=1, keepdims=True)
    target = jnp.right_shift(lax.broadcasted_iota(jnp.int32, (SLOTS, LANES), 1), 1).astype(F32)
    main, spare = slot_maps(start, count, target, 0.5)
    fmap[0] = main
    fmap[1] = spare
    low, high = encode(main, spare, frames[...])
    place = jnp.bitwise_and(lax.broadcasted_iota(jnp.int32, high.shape, 0), SLOT - 1)
    in_spare = lax.broadcasted_iota(jnp.int32, high.shape, 1) >= 64
    high = jnp.where((place >= 10) & in_spare, count, high)
    slots[:, 0:256] = low.astype(BF16)
    slots[:, 256:384] = high.astype(BF16)
    ygat[t, 0:SLOT, :] = slots[0:SLOT, :]

    def z_relay(stage):
        for direction in (0, 1):
            if reaches(direction, 2 * stage + 2):
                z_landed(direction, 2 * stage + 2)
                z_sends(direction, 2 * stage + 2)

    def seq_sends(stage):
        for direction in (0, 1):
            z_landed(direction, 2 * stage + 1)
            for way in (0, 1):
                x_copy(way, direction, stage).start()
            core_copy(0, direction, stage, core).start()

    def pooled_sends(kind):
        each_of(kind, lambda step: pooled_copy(step).start())

    def x_relay(stage):
        for direction in (0, 1):
            for way in (0, 1):
                x_landed(way, direction, stage)
                x_onward(way, direction, stage).start()
                core_copy(3 if way == 0 else 1, direction, stage, core).start()

    def far_relay(stage):
        for direction in (0, 1):
            for way in (0, 1):
                far_landed(way, direction, stage)
            core_copy(2, direction, stage, core).start()

    def from_core(step):
        for direction in (0, 1):
            for stage in range(STAGES):
                core_copy(step, direction, stage, 1 - core).wait_recv()

    def part_sem(step, kind):
        return step * CLASSES + kind

    def part_copy(step, kind):
        ref = ygat.at[t, pl.ds(kind * GROUP, GROUP), :]
        return pltpu.make_async_remote_copy(
            src_ref=ref, dst_ref=ref, send_sem=ys.at[part_sem(step, kind)], recv_sem=yr.at[part_sem(step, kind)],
            device_id={"tp": tp_at(step)}, device_id_type=MESH,
        )

    def part_landed(step, kind):
        ref = ygat.at[tp_at(N_TP - step), pl.ds(kind * GROUP, GROUP), :]
        return pltpu.make_async_remote_copy(
            src_ref=ref, dst_ref=ref, send_sem=ys.at[part_sem(step, kind)], recv_sem=yr.at[part_sem(step, kind)],
            device_id={"tp": tp_at(step)}, device_id_type=MESH,
        )

    def pass_on(kind):
        each_of((4 - kind) % 4, lambda step: pooled_landed(step).wait_recv())
        for step in (2, 1, 3):
            part_copy(step, kind).start()

    pooled_sends(0)
    z_relay(0)
    pooled_sends(3)
    seq_sends(0)
    z_relay(1)
    pooled_sends(2)
    pooled_sends(1)
    seq_sends(1)
    locals_in[0].start()
    locals_in[1].start()
    z_relay(2)
    seq_sends(2)
    locals_in[2].start()
    locals_in[3].start()
    x_relay(0)
    pass_on(0)
    pass_on(1)
    z_relay(3)
    seq_sends(3)
    x_relay(1)
    pass_on(2)
    x_relay(2)
    pass_on(3)
    far_relay(0)

    slot = lax.broadcasted_iota(jnp.int32, (SLOTS, SLOTS), 0)
    source = lax.broadcasted_iota(jnp.int32, (SLOTS, SLOTS), 1)
    last = jnp.bitwise_and(source, SLOT - 1) == SLOT - 1
    slot_of = jnp.bitwise_and(distance(jnp.right_shift(slot, 4)) + e, N_ENC - 1)
    source_of = jnp.bitwise_and(distance(jnp.right_shift(source, 4)) + e, N_ENC - 1)
    same = jnp.where((slot_of == source_of) & last, 1.0, 0.0).astype(BF16)
    before = jnp.where((source_of < slot_of) & last, 1.0, 0.0).astype(BF16)
    marks = ygat[t, :, 256:384]
    end_lane = lax.broadcasted_iota(jnp.int32, (SLOTS, 128), 1) == 127
    count = jnp.sum(jnp.where(end_lane, nn(same, marks), 0.0), axis=1, keepdims=True)
    start = jnp.sum(jnp.where(end_lane, nn(before, marks), 0.0), axis=1, keepdims=True)
    first = offset[0].astype(F32)
    end = jnp.max(start + count, axis=0, keepdims=True) + first
    target = lax.broadcasted_iota(jnp.int32, (SLOTS, LANES), 1).astype(F32) - first
    main, spare = slot_maps(start, count, target, 1.0)
    tmap[0] = main
    tmap[1] = spare

    x_relay(3)
    far_relay(1)

    eye = identity(LANES)

    def unpack(step):
        if step:
            for kind in range(CLASSES):
                part_landed(step, kind).wait_recv()
        part = tp_at(N_TP - step)
        rows = decode(ygat[part], tmap[0], tmap[1], eye).astype(BF16)
        for index in range(N_TP):
            place = lax.rem(part * N_TP + index + N_ENC - e, N_ENC)
            chunk = pl.ds(pl.multiple_of(place * CHUNK, CHUNK), CHUNK)
            turned[chunk, :] = rows[index * CHUNK : index * CHUNK + CHUNK]

    unpack(0)
    unpack(1)
    far_relay(2)
    unpack(3)
    unpack(2)
    pooled[...] = nt(eye, turned[...]).astype(BF16)

    sums[...] = jnp.zeros_like(sums)

    def forward(step, which):
        cols = pl.ds(slab_at(step, which), SLAB)
        projected = nn(pooled[0:TOKENS, :], wfull[:, cols]).astype(BF16).astype(F32)
        token = lax.broadcasted_iota(jnp.int32, projected.shape, 0).astype(F32)
        hidden = jnp.where((token >= first) & (token < end), projected, textv[:, cols].astype(F32))
        hid[:, cols] = hidden.astype(BF16)
        squares = hidden * hidden
        slopes = cotv[:, cols].astype(F32) * gain[:, cols] * hidden
        sums[0, 0:TOKENS, :] += squares[:, 0:128] + squares[:, 128:256]
        sums[1, 0:TOKENS, :] += slopes[:, 0:128] + slopes[:, 128:256]

    for copy in locals_in:
        copy.wait()
    forward(0, core)
    far_relay(3)
    forward(1, core)
    forward(3, core)
    for step in (0, 1, 3):
        from_core(step)
        forward(step, 1 - core)
    forward(2, core)
    from_core(2)
    forward(2, 1 - core)

    stats[0] = jnp.zeros((8, LANES), F32)
    stats[0, 0:1, :] = jnp.sum(jnp.transpose(sums[0]), axis=0, keepdims=True)
    stats[0, 1:2, :] = jnp.sum(jnp.transpose(sums[1]), axis=0, keepdims=True)

    def stat_copy(step):
        return pltpu.make_async_remote_copy(
            src_ref=stats.at[0], dst_ref=stats.at[step], send_sem=ss.at[step], recv_sem=sr.at[step],
            device_id={"tp": tp_at(step)}, device_id_type=MESH,
        )

    for step in (2, 1, 3):
        stat_copy(step).start()
    gh[TOKENS:LANES, :] = jnp.zeros((LANES - TOKENS, WIDE), BF16)
    for direction in (0, 1):
        for stage in range(STAGES):
            for step in (1, 2):
                if reaches(direction, 2 * stage + step):
                    z_copy(direction, 2 * stage, step).wait_send()
            for way in (0, 1):
                x_copy(way, direction, stage).wait_send()
                x_onward(way, direction, stage).wait_send()
            for step in range(N_X):
                core_copy(step, direction, stage, core).wait_send()

    for step in (2, 1, 3):
        stat_copy(step).wait_recv()
    total = (stats[0] + stats[1]) + (stats[2] + stats[3])
    inv_row = lax.rsqrt(total[0:1] / D + EPS)
    slope_row = total[1:2] / D
    inv = column(inv_row, LANES)[0:TOKENS]
    back = column(inv_row * inv_row * inv_row * slope_row, LANES)[0:TOKENS]
    inv = jnp.concatenate([inv, inv], axis=1)
    back = jnp.concatenate([back, back], axis=1)

    def backward(index):
        cols = pl.ds(pl.multiple_of(index * SLAB, SLAB), SLAB)
        hidden = hid[:, cols].astype(F32)
        weighted = cotv[:, cols].astype(F32) * gain[:, cols]
        gh[0:TOKENS, cols] = (inv * weighted - back * hidden).astype(BF16)

    def normed(index):
        cols = pl.ds(pl.multiple_of(index * SLAB, SLAB), SLAB)
        mixv[:, cols] = (hid[:, cols].astype(F32) * inv * gain[:, cols]).astype(BF16)

    each(0, WIDE // SLAB, backward)

    def sum_copy(step, kind):
        rows = pl.ds(kind * GROUP, GROUP)
        return pltpu.make_async_remote_copy(
            src_ref=ysend.at[step, rows, :], dst_ref=yrecv.at[step, rows, :],
            send_sem=rs.at[part_sem(step, kind)], recv_sem=rr.at[part_sem(step, kind)],
            device_id={"tp": tp_at(step)}, device_id_type=MESH,
        )

    def back_copy(step):
        return pltpu.make_async_remote_copy(
            src_ref=bsend.at[slot_rows(place_of(step)), :], dst_ref=bret.at[slot_rows(place_of(N_ENC - step)), :],
            send_sem=gs.at[step], recv_sem=gr.at[step], device_id={"enc": enc_at(step)}, device_id_type=MESH,
        )

    def back_landed(step):
        ref = bret.at[slot_rows(place_of(N_ENC - step)), :]
        return pltpu.make_async_remote_copy(
            src_ref=ref, dst_ref=ref, send_sem=gs.at[step], recv_sem=gr.at[step],
            device_id={"enc": enc_at(step)}, device_id_type=MESH,
        )

    main, spare = tmap[0], tmap[1]

    def partial(step):
        places = [lax.rem(tp_at(step) * N_TP + index + N_ENC - e, N_ENC) for index in range(N_TP)]
        chunks = [wfull[pl.ds(pl.multiple_of(place * CHUNK, CHUNK), CHUNK), :] for place in places]
        low, high = encode(main, spare, nt(jnp.concatenate(chunks, axis=0), gh[...]).astype(BF16))
        ysend[step, :, 0:256] = low.astype(BF16)
        ysend[step, :, 256:384] = high.astype(BF16)

    for step in (2, 1, 3):
        partial(step)
        for kind in (0, 1):
            sum_copy(step, kind).start()
    for step in (2, 1, 3):
        sum_copy(step, 2).start()
    partial(0)
    each(0, WIDE // SLAB, normed)
    for step in (2, 1, 3):
        sum_copy(step, 3).start()
    mixed_out = pltpu.make_async_copy(mixv, mixed, ls.at[3])
    mixed_out.start()

    for kind in range(CLASSES):
        rows = slice(kind * GROUP, kind * GROUP + GROUP)
        for step in (2, 1, 3):
            sum_copy(step, kind).wait_recv()
        near = ysend[0, rows, :].astype(F32) + yrecv[1, rows, :].astype(F32)
        far = yrecv[2, rows, :].astype(F32) + yrecv[3, rows, :].astype(F32)
        bsend[rows, :] = (near + far).astype(BF16)
        each_of(kind, lambda step: back_copy(step).start())
    bret[0:SLOT, :] = bsend[0:SLOT, :]

    each(1, N_ENC, lambda step: pooled_copy(step).wait_send())
    for step in range(1, N_TP):
        stat_copy(step).wait_send()
        for kind in range(CLASSES):
            part_copy(step, kind).wait_send()

    for step in range(1, N_TP):
        for kind in range(CLASSES):
            sum_copy(step, kind).wait_send()
    each(1, N_ENC, lambda step: back_landed(step).wait_recv())
    grads[...] = decode(bret[...], fmap[0], fmap[1], identity(LANES)).astype(BF16)
    each(1, N_ENC, lambda step: back_copy(step).wait_send())
    mixed_out.wait()


def body(frames, proj_weight, text_emb, norm_gain, cotangent, counts, offsets):
    any_space = pl.BlockSpec(memory_space=pl.ANY)
    vmem = pl.BlockSpec(memory_space=pltpu.VMEM)
    smem = pl.BlockSpec(memory_space=pltpu.SMEM)
    dma = pltpu.SemaphoreType.DMA
    mixed, grads = pl.pallas_call(
        kernel,
        out_shape=(
            jax.ShapeDtypeStruct((TOKENS, WIDE), BF16),
            jax.ShapeDtypeStruct((PART, LANES), BF16),
        ),
        in_specs=[any_space] * 6 + [smem],
        out_specs=(any_space, vmem),
        scratch_shapes=[
            pltpu.VMEM((PART, LANES), BF16),
            pltpu.VMEM((1, WIDE), F32),
            pltpu.VMEM((1, N_ENC), jnp.int32),
            pltpu.VMEM((N_ENC * CHUNK, WIDE), BF16),
            pltpu.VMEM((TOKENS, WIDE), BF16),
            pltpu.VMEM((TOKENS, WIDE), BF16),
            pltpu.VMEM((TOKENS, WIDE), BF16),
            pltpu.VMEM((LANES, WIDE), BF16),
            pltpu.VMEM((TOKENS, WIDE), BF16),
            pltpu.VMEM((N_ENC * CHUNK, LANES), BF16),
            pltpu.VMEM((LANES, N_ENC * CHUNK), BF16),
            pltpu.VMEM((SLOTS, LANES), BF16),
            pltpu.VMEM((N_TP, SLOTS, LANES), BF16),
            pltpu.VMEM((N_TP, SLOTS, LANES), BF16),
            pltpu.VMEM((N_TP, SLOTS, LANES), BF16),
            pltpu.VMEM((N_TP, 8, LANES), F32),
            pltpu.VMEM((2, LANES, 128), F32),
            pltpu.VMEM((SLOTS, LANES), BF16),
            pltpu.VMEM((SLOTS, LANES), BF16),
            pltpu.VMEM((2, SLOTS, LANES), BF16),
            pltpu.VMEM((2, SLOTS, LANES), BF16),
            *[dma((4 * STAGES,)) for _ in range(6)],
            *[dma((8 * STAGES,)) for _ in range(2)],
            *[dma((N_ENC,)) for _ in range(2)],
            *[dma((N_TP * CLASSES,)) for _ in range(2)],
            *[dma((N_TP,)) for _ in range(2)],
            *[dma((N_TP * CLASSES,)) for _ in range(2)],
            *[dma((N_ENC,)) for _ in range(2)],
            dma((7,)),
        ],
        compiler_params=pltpu.CompilerParams(
            collective_id=0, has_side_effects=True, vmem_limit_bytes=56 * 1024 * 1024
        ),
    )(frames.T, proj_weight, text_emb, norm_gain.reshape(1, WIDE), cotangent, counts, offsets)
    return mixed, grads.T


def solution(mesh):
    in_specs = (
        P(("enc", "seq"), "tp"),
        P("enc", "tp"),
        P(("enc", "seq"), "tp"),
        P("tp"),
        P(("enc", "seq"), "tp"),
        P(("enc", "seq"), None),
        P(("enc", "seq")),
    )
    out_specs = (P(("enc", "seq"), "tp"), P(("enc", "seq"), "tp"))
    return jax.shard_map(body, mesh=mesh, in_specs=in_specs, out_specs=out_specs, check_vma=False)
```
